32 devices in a mesh: dp: 4 (over y, x), row: 2 (over core), col: 4 (over z).
Axes of the slice: x: 2, y: 2, z: 4, core: 2. Of those that a mesh axis runs over, the one named last changes fastest.
Arguments:
- tokens: bfloat16 [1024, 4096], P('dp', 'col'), may hold values from -6 to 6
- cotangent: bfloat16 [1024, 4096], P('dp', 'col'), may hold values from -6 to 6
- counts: int32 [4], P('dp'), may hold values from 1 to 4, as said below
- up_blocks: bfloat16 [4, 2, 128, 128, 128], P('col', 'row'), may hold values from -0.1875 to 0.1875
- up_rows: int32 [4, 2, 128], P('col', 'row'), may hold values from 0 to 7, as said below
- up_cols: int32 [4, 2, 128], P('col', 'row'), may hold values from 0 to 63, as said below
- down_blocks: bfloat16 [2, 4, 128, 128, 128], P('row', 'col'), may hold values from -0.09375 to 0.09375
- down_rows: int32 [2, 4, 128], P('row', 'col'), may hold values from 0 to 63, as said below
- down_cols: int32 [2, 4, 128], P('row', 'col'), may hold values from 0 to 7, as said below
Outputs:
- y_out: bfloat16 [1024, 4096], P('dp', 'col')
- grad_tokens: bfloat16 [1024, 4096], P('dp', 'col')
- grad_up: float32 [4, 2, 128, 128, 128], P('col', 'row', 'dp')
- grad_down: float32 [2, 4, 128, 128, 128], P('row', 'col', 'dp')
The draws below stay inside these ranges and needn't reach their ends.
Inputs may be any that keep to these rules, and one draw needn't show every extreme that they name: Replica d has counts[d] live microbatches of 64 tokens in its first slots; the rest of its 4 slots are padding. `up_rows`: within each tile the 128 blocks stand at distinct positions, and every tile holds its block (0, 0) and its block (7, 63). `up_cols`: paired with up_rows as above. `down_rows`: within each tile the 128 blocks stand at distinct positions, and every tile holds its block (0, 0) and its block (63, 7). `down_cols`: paired with down_rows as above.
All inputs are finite; a program needn't handle non-finite values.
Results may differ from the reference program's by a relative error of at most 0.029.
Values may be sent and summed in bfloat16 or wider, within the bound.
No kernel may reach another device: no remote copies, remote signals or barrier semaphores. Data moves between devices by JAX's collectives and lax.ppermute only.
A program may use at most 128 MiB of HBM per device.

```python
import jax
import jax.numpy as jnp
from jax import lax

D = 4096
FF = 16384
BLOCK = 128
MB_TOK = 64
MB_MAX = 4
CAP = 256
TOKENS = 1024
TILE_D = 8
TILE_F = 64
NB = 128
N_DP = 4
N_ROW = 2
N_COL = 4


def tile_pattern(key, tile_count, row_cells, col_cells, block_count):
    cell_count = row_cells * col_cells
    tile_keys = jax.random.split(key, tile_count)

    def one_tile(tile_key):
        first_key, second_key = jax.random.split(tile_key)
        middle = jax.random.permutation(first_key, cell_count - 2)[:block_count - 2].astype(jnp.int32) + 1
        chosen = jnp.concatenate([jnp.zeros((1,), jnp.int32), middle, jnp.full((1,), cell_count - 1, jnp.int32)])
        shuffle = jax.random.permutation(second_key, block_count)
        chosen = chosen[shuffle]
        return (chosen // col_cells, chosen % col_cells)
    return jax.vmap(one_tile)(tile_keys)


def draw_up_rows(key, part):
    block_rows, block_cols = tile_pattern(jax.random.fold_in(key, 11), N_COL * N_ROW, TILE_D, TILE_F, NB)
    return block_rows.reshape(N_COL, N_ROW, NB).astype(jnp.int32)


def draw_up_cols(key, part):
    block_rows, block_cols = tile_pattern(jax.random.fold_in(key, 11), N_COL * N_ROW, TILE_D, TILE_F, NB)
    return block_cols.reshape(N_COL, N_ROW, NB).astype(jnp.int32)


def draw_down_rows(key, part):
    block_rows, block_cols = tile_pattern(jax.random.fold_in(key, 23), N_ROW * N_COL, TILE_F, TILE_D, NB)
    return block_rows.reshape(N_ROW, N_COL, NB).astype(jnp.int32)


def draw_down_cols(key, part):
    block_rows, block_cols = tile_pattern(jax.random.fold_in(key, 23), N_ROW * N_COL, TILE_F, TILE_D, NB)
    return block_cols.reshape(N_ROW, N_COL, NB).astype(jnp.int32)


def draw_counts(key, part):
    key_one, key_two, key_three, key_four = jax.random.split(jax.random.fold_in(key, 37), 4)
    busy_flag = jax.random.randint(key_one, (N_DP,), 0, 4) == 0
    extra_count = jax.random.randint(key_two, (N_DP,), 2, MB_MAX + 1)
    micro_counts = jnp.where(busy_flag, extra_count, 1).astype(jnp.int32)
    top_index = jax.random.randint(key_three, (), 0, N_DP)
    low_index = (top_index + jax.random.randint(key_four, (), 1, N_DP)) % N_DP
    micro_counts = micro_counts.at[top_index].set(MB_MAX)
    micro_counts = micro_counts.at[low_index].set(1)
    return micro_counts


def block_scale(rng, extent, pieces, smallest, largest):
    loudness = 1.0
    for dim, parts in pieces:
        steps = jax.random.uniform(jax.random.fold_in(jax.random.fold_in(rng, 6), dim), (parts,), jnp.float32, smallest / len(pieces), largest / len(pieces))
        loudness = loudness * jnp.repeat(jnp.exp(steps), extent[dim] // parts).reshape((-1,) + (1,) * (len(extent) - 1 - dim))
    return loudness


def gaussian(key, dims, spread, limit, pieces=(), held_as=jnp.bfloat16):
    array = spread * jax.random.normal(key, dims, jnp.float32)
    if pieces:
        array = array * block_scale(key, dims, pieces, -0.22, 0.18)
    return jnp.clip(array, -limit, limit).astype(held_as)


def setup_inputs(seed: int = 0) -> dict:
    seeds = jax.random.split(jax.random.key(seed), 10)
    return {
        "tokens": gaussian(seeds[0], (TOKENS, D), 1.0, 6.0, ((0, 4), (1, 4))),
        "cotangent": gaussian(seeds[1], (TOKENS, D), 1.0, 6.0, ((0, 4), (1, 4))),
        "counts": draw_counts(jax.random.fold_in(seeds[9], 71), 0),
        "up_blocks": gaussian(seeds[3], (N_COL, N_ROW, NB, BLOCK, BLOCK), (D // 4) ** -0.5, 0.1875, ((0, 4), (1, 2))),
        "up_rows": draw_up_rows(jax.random.fold_in(seeds[9], 71), 0),
        "up_cols": draw_up_cols(jax.random.fold_in(seeds[9], 71), 0),
        "down_blocks": gaussian(seeds[6], (N_ROW, N_COL, NB, BLOCK, BLOCK), (FF // 4) ** -0.5, 0.09375, ((0, 2), (1, 4))),
        "down_rows": draw_down_rows(jax.random.fold_in(seeds[9], 71), 0),
        "down_cols": draw_down_cols(jax.random.fold_in(seeds[9], 71), 0),
    }


def wire_round(values):
    return lax.optimization_barrier(values.astype(jnp.bfloat16)).astype(jnp.float32)


def gelu_exact(hidden_in):
    return 0.5 * hidden_in * (1.0 + jax.scipy.special.erf(hidden_in * 0.7071067811865476))


def gelu_slope(hidden_in):
    normal_cdf = 0.5 * (1.0 + jax.scipy.special.erf(hidden_in * 0.7071067811865476))
    return normal_cdf + hidden_in * jnp.exp(-0.5 * hidden_in * hidden_in) * 0.3989422804014327


def tile_product(operand, blocks, in_index, out_index, out_count, flipped):
    row_count = operand.shape[0]
    selected = jnp.take(operand.reshape(row_count, -1, BLOCK), in_index, axis=1).astype(jnp.float32)
    pattern = "tnj,nkj->tnk" if flipped else "tnk,nkj->tnj"
    products = jnp.einsum(pattern, selected, blocks.astype(jnp.float32))
    placing = (out_index[:, None] == jnp.arange(out_count, dtype=jnp.int32)[None, :]).astype(jnp.float32)
    combined = jnp.einsum("tnj,nb->tbj", products, placing)
    return combined.reshape(row_count, out_count * BLOCK)


def block_terms(left_side, right_side, left_index, right_index):
    left_slab = jnp.take(left_side.reshape(TOKENS, -1, BLOCK), left_index, axis=1).astype(jnp.float32)
    right_slab = jnp.take(right_side.reshape(TOKENS, -1, BLOCK), right_index, axis=1).astype(jnp.float32)
    return jnp.einsum("tnk,tnj->nkj", left_slab, right_slab)


def reference(tokens, cotangent, counts, up_blocks, up_rows, up_cols, down_blocks, down_rows, down_cols):
    width_cols = TILE_D * BLOCK
    hidden_cols = TILE_F * BLOCK
    position = jnp.arange(TOKENS, dtype=jnp.int32)
    replica = position // CAP
    micro_slot = (position % CAP) // MB_TOK
    live_rows = (micro_slot < jnp.take(counts, replica)).astype(jnp.float32)[:, None]
    total_count = jnp.sum(counts).astype(jnp.float32)

    hidden_pieces = []
    for row_index in range(N_ROW):
        summed = jnp.zeros((TOKENS, hidden_cols), jnp.float32)
        for col_index in range(N_COL):
            operand = tokens[:, col_index * width_cols:(col_index + 1) * width_cols]
            summed = summed + wire_round(tile_product(operand, up_blocks[col_index, row_index], up_rows[col_index, row_index], up_cols[col_index, row_index], TILE_F, False))
        hidden_pieces.append(summed)
    hidden = jnp.concatenate(hidden_pieces, axis=1)
    activation = gelu_exact(hidden).astype(jnp.bfloat16)

    output_pieces = []
    for col_index in range(N_COL):
        summed = jnp.zeros((TOKENS, width_cols), jnp.float32)
        for row_index in range(N_ROW):
            operand = activation[:, row_index * hidden_cols:(row_index + 1) * hidden_cols]
            summed = summed + wire_round(tile_product(operand, down_blocks[row_index, col_index], down_rows[row_index, col_index], down_cols[row_index, col_index], TILE_D, False))
        output_pieces.append(summed)
    y_out = (jnp.concatenate(output_pieces, axis=1) * live_rows).astype(jnp.bfloat16)

    grad_mask = cotangent * live_rows.astype(jnp.bfloat16)
    act_pieces = []
    for row_index in range(N_ROW):
        summed = jnp.zeros((TOKENS, hidden_cols), jnp.float32)
        for col_index in range(N_COL):
            operand = grad_mask[:, col_index * width_cols:(col_index + 1) * width_cols]
            summed = summed + wire_round(tile_product(operand, down_blocks[row_index, col_index], down_cols[row_index, col_index], down_rows[row_index, col_index], TILE_F, True))
        act_pieces.append(summed)
    act_grad = jnp.concatenate(act_pieces, axis=1)
    hidden_grad = (act_grad * gelu_slope(hidden)).astype(jnp.bfloat16)

    input_pieces = []
    for col_index in range(N_COL):
        summed = jnp.zeros((TOKENS, width_cols), jnp.float32)
        for row_index in range(N_ROW):
            operand = hidden_grad[:, row_index * hidden_cols:(row_index + 1) * hidden_cols]
            summed = summed + wire_round(tile_product(operand, up_blocks[col_index, row_index], up_cols[col_index, row_index], up_rows[col_index, row_index], TILE_D, True))
        input_pieces.append(summed)
    grad_tokens = jnp.concatenate(input_pieces, axis=1).astype(jnp.bfloat16)

    up_list = []
    for col_index in range(N_COL):
        inner = []
        for row_index in range(N_ROW):
            left_side = tokens[:, col_index * width_cols:(col_index + 1) * width_cols]
            right_side = hidden_grad[:, row_index * hidden_cols:(row_index + 1) * hidden_cols]
            inner.append(block_terms(left_side, right_side, up_rows[col_index, row_index], up_cols[col_index, row_index]) / total_count)
        up_list.append(jnp.stack(inner))
    grad_up = jnp.stack(up_list)

    down_list = []
    for row_index in range(N_ROW):
        inner = []
        for col_index in range(N_COL):
            left_side = activation[:, row_index * hidden_cols:(row_index + 1) * hidden_cols]
            right_side = grad_mask[:, col_index * width_cols:(col_index + 1) * width_cols]
            inner.append(block_terms(left_side, right_side, down_rows[row_index, col_index], down_cols[row_index, col_index]) / total_count)
        down_list.append(jnp.stack(inner))
    grad_down = jnp.stack(down_list)
    return (y_out, grad_tokens, grad_up, grad_down)
```

```python
import functools

import jax
import jax.numpy as jnp
from jax import lax
from jax.experimental import pallas as pl
from jax.experimental.pallas import tpu as pltpu
from jax.sharding import PartitionSpec as P

FF = 16384
MB_TOK = 64
MB_MAX = 4
UNIT = 16
BATCH = 8
GROUP = 16
VMEM_LIMIT = 48 * 1024 * 1024
CAPACITIES = (4, 8, 12)

SMEM = pl.BlockSpec(memory_space=pltpu.SMEM)
VMEM = pl.BlockSpec(memory_space=pltpu.VMEM)

INWARD = [(0, 1), (3, 2)]
MIDDLE = [(1, 2), (2, 1)]
OUTWARD = [(1, 0), (2, 3)]


def gelu_exact(hidden_in):
    return 0.5 * hidden_in * (1.0 + lax.erf(hidden_in * 0.7071067811865476))


def gelu_slope(hidden_in):
    normal_cdf = 0.5 * (1.0 + lax.erf(hidden_in * 0.7071067811865476))
    return normal_cdf + hidden_in * jnp.exp(-0.5 * hidden_in * hidden_in) * 0.3989422804014327


def bits_of(size):
    return [1 << i for i in range(size.bit_length() - 1)]


def submasks(bits):
    out = [0]
    for b in bits:
        out = out + [m | b for m in out]
    return out


def swap(x, axis, mask):
    size = lax.axis_size(axis)
    return lax.ppermute(x, axis, [(i, i ^ mask) for i in range(size)])


def params():
    return pltpu.CompilerParams(vmem_limit_bytes=VMEM_LIMIT)


def cost(flops, moved):
    return pl.CostEstimate(flops=flops, bytes_accessed=moved, transcendentals=0)


def slot_of(index, side, count):
    moved = index + side * (count // 2)
    return jnp.where(moved >= count, moved - count, moved)


def lanes(ref, index, block):
    return ref[:, pl.ds(pl.multiple_of(index * block, block), block)]


def block_dot(a, w, flipped):
    return lax.dot_general(
        a, w, (((1,), (1 if flipped else 0,)), ((), ())), preferred_element_type=jnp.float32
    )


def spread_kernel(th, group, flipped, meta, take, put, x_ref, w_ref, far_ref, near_ref, acc):
    g = pl.program_id(0)
    block = w_ref.shape[-1]
    half = th // 2
    side = meta[0]

    @pl.when(g == 0)
    def _():
        acc[...] = jnp.zeros_like(acc)

    step = min(BATCH, group)
    for s in range(group // step):
        products = []
        for j in range(step):
            a = lanes(x_ref, take[g * group + s * step + j], block)
            products.append(block_dot(a, w_ref[s * step + j], flipped))
        for j in range(step):
            o = slot_of(put[g * group + s * step + j], side, th)
            acc[o] += products[j]

    @pl.when(g == pl.num_programs(0) - 1)
    def _():
        far_ref[...] = acc[:half].astype(jnp.bfloat16)
        near_ref[...] = acc[half:].astype(jnp.bfloat16)


def spread(meta, x, blocks, take, put, th, flipped):
    rows, width = x.shape
    nb, block, _ = blocks.shape
    group = min(GROUP, nb)
    shape = jax.ShapeDtypeStruct((th // 2, rows, block), jnp.bfloat16)
    whole = pl.BlockSpec((th // 2, rows, block), lambda g, *_: (0, 0, 0))
    return pl.pallas_call(
        functools.partial(spread_kernel, th, group, flipped),
        out_shape=(shape, shape),
        grid_spec=pltpu.PrefetchScalarGridSpec(
            num_scalar_prefetch=3,
            grid=(nb // group,),
            in_specs=[
                pl.BlockSpec((rows, width), lambda g, *_: (0, 0)),
                pl.BlockSpec((group, block, block), lambda g, *_: (g, 0, 0)),
            ],
            out_specs=(whole, whole),
            scratch_shapes=[pltpu.VMEM((th, rows, block), jnp.float32)],
        ),
        compiler_params=params(),
        cost_estimate=cost(8 * nb * rows * block * block, nb * block * block * 2),
    )(meta, take, put, x, blocks)


def collect_kernel(th, tw, pieces, group, flipped, parts, meta, take, put, *refs):
    h_refs = refs[:parts]
    w_ref = refs[parts]
    out_refs = refs[parts + 1 : parts + 1 + pieces]
    acc = refs[-1]
    g = pl.program_id(0)
    side, me = meta[0], meta[1]

    @pl.when(g == 0)
    def _():
        acc[...] = jnp.zeros_like(acc)

    step = min(BATCH, group)
    for s in range(group // step):
        products = []
        for j in range(step):
            i = slot_of(take[g * group + s * step + j], side, th)
            a = jnp.concatenate([h[i] for h in h_refs], axis=0)
            products.append(block_dot(a, w_ref[s * step + j], flipped))
        for j in range(step):
            acc[put[g * group + s * step + j]] += products[j]

    @pl.when(g == pl.num_programs(0) - 1)
    def _():
        each = tw // pieces
        block = w_ref.shape[-1]
        for q in range(pieces):
            base = jnp.bitwise_xor(me, q) * each
            for t in range(each):
                out_refs[q][:, t * block : (t + 1) * block] = acc[base + t].astype(jnp.bfloat16)


def collect(meta, hs, blocks, take, put, tw, pieces, flipped):
    th, _, block = hs[0].shape
    rows = sum(h.shape[1] for h in hs)
    nb = blocks.shape[0]
    group = min(GROUP, nb)
    shape = jax.ShapeDtypeStruct((rows, tw * block // pieces), jnp.bfloat16)
    whole = pl.BlockSpec((rows, tw * block // pieces), lambda g, *_: (0, 0))
    return pl.pallas_call(
        functools.partial(collect_kernel, th, tw, pieces, group, flipped, len(hs)),
        out_shape=(shape,) * pieces,
        grid_spec=pltpu.PrefetchScalarGridSpec(
            num_scalar_prefetch=3,
            grid=(nb // group,),
            in_specs=[pl.BlockSpec(h.shape, lambda g, *_: (0, 0, 0)) for h in hs]
            + [pl.BlockSpec((group, block, block), lambda g, *_: (g, 0, 0))],
            out_specs=(whole,) * pieces,
            scratch_shapes=[pltpu.VMEM((tw, rows, block), jnp.float32)],
        ),
        compiler_params=params(),
        cost_estimate=cost(8 * nb * rows * block * block, nb * block * block * 2),
    )(meta, take, put, *hs, blocks)


def grads_kernel(th, nb, size, orders, level, parts, hidden_left, meta, take, put, total, *refs):
    left = refs[:parts]
    right = refs[parts : 2 * parts]
    got = refs[2 * parts : 2 * parts + 2 * level]
    outs = refs[2 * parts + 2 * level :]
    side, me = meta[0], meta[2]
    share = nb // size
    each = share // 2
    step = min(BATCH, each)
    block = outs[0].shape[-1]
    last = level == len(orders[0])

    def side_rows(group, hidden, index):
        if hidden:
            i = slot_of(index, side, th)
            return jnp.concatenate([h[i] for h in group], axis=0)
        return jnp.concatenate([lanes(x, index, block) for x in group], axis=0)

    for half in range(2):
        order = orders[half]
        if last:
            masks = [0]
        else:
            masks = [order[level] | m for m in submasks(order[level + 1 :])]
        for entry, mask in enumerate(masks):
            owner = jnp.bitwise_xor(me, mask)

            def run(b, carry, half=half, order=order, entry=entry, mask=mask, owner=owner):
                products = []
                for j in range(step):
                    k = owner * share + half * each + b * step + j
                    a = side_rows(left, hidden_left, take[k])
                    c = side_rows(right, not hidden_left, put[k])
                    products.append(
                        lax.dot_general(
                            a, c, (((0,), (0,)), ((), ())), preferred_element_type=jnp.float32
                        )
                    )
                for j in range(step):
                    value = products[j]
                    for i in range(level):
                        at = submasks(order[i + 1 :]).index(mask)
                        value = value + got[2 * i + half][at * each + b * step + j].astype(
                            jnp.float32
                        )
                    if last:
                        outs[0][half * each + b * step + j] = value / total[0]
                    else:
                        outs[half][entry * each + b * step + j] = value.astype(jnp.bfloat16)
                return carry

            lax.fori_loop(0, each // step, run, 0)


def grads(meta, left, right, hidden_left, take, put, total, got, level, size, orders, th):
    nb = take.shape[0]
    block = (left if hidden_left else right)[0].shape[-1]
    each = nb // size // 2
    last = level == len(orders[0])
    if last:
        count = 2 * each
        out_shape = jax.ShapeDtypeStruct((2 * each, block, block), jnp.float32)
    else:
        entries = 1 << (len(orders[0]) - level - 1)
        count = 2 * entries * each
        shape = jax.ShapeDtypeStruct((entries * each, block, block), jnp.bfloat16)
        out_shape = (shape, shape)
    flat = [r for pair in got for r in pair]
    return pl.pallas_call(
        functools.partial(grads_kernel, th, nb, size, orders, level, len(left), hidden_left),
        out_shape=out_shape,
        in_specs=[SMEM] * 4 + [VMEM] * (2 * len(left) + len(flat)),
        out_specs=VMEM if last else (VMEM, VMEM),
        compiler_params=params(),
        cost_estimate=cost(8 * count * 128 * block * block, count * block * block * 4),
    )(meta, take, put, total, *left, *right, *flat)


def reduce_grads(meta, left, right, hidden_left, take, put, total, size, th):
    bits = bits_of(size)
    orders = (bits, bits[1:] + bits[:1])
    got = []
    for level in range(len(bits)):
        send = grads(meta, left, right, hidden_left, take, put, total, got, level, size, orders, th)
        got.append(tuple(swap(send[h], "dp", orders[h][level]) for h in range(2)))
    return grads(
        meta, left, right, hidden_left, take, put, total, got, len(bits), size, orders, th
    )


def lend_kernel(cap_units, slots, plan, tok, cot, tok_out, cot_out):
    width = tok_out.shape[1]
    spare, first, me = plan[1], plan[2], plan[5]
    units = (tok.shape[0] - MB_TOK) // UNIT
    column = pl.multiple_of(me * width, width)
    for j in range(slots):
        own = jnp.logical_and(j >= first, j < first + spare)
        unit = jnp.clip(cap_units + j - first, 0, units - 1)
        start = pl.multiple_of(MB_TOK + unit * UNIT, UNIT)
        for src, dst in ((tok, tok_out), (cot, cot_out)):
            rows = src[pl.ds(start, UNIT), pl.ds(column, width)]
            dst[j * UNIT : (j + 1) * UNIT, :] = jnp.where(own, rows, jnp.zeros_like(rows))


def lend(plan, tok, cot, cap_units, slots, pieces):
    shape = jax.ShapeDtypeStruct((slots * UNIT, tok.shape[1] // pieces), jnp.bfloat16)
    return pl.pallas_call(
        functools.partial(lend_kernel, cap_units, slots),
        out_shape=(shape, shape),
        in_specs=[SMEM, VMEM, VMEM],
        out_specs=(VMEM, VMEM),
        compiler_params=params(),
        cost_estimate=cost(0, tok.size * 4),
    )(plan, tok, cot)


def borrow_kernel(cap_units, pieces, plan, tok, cot, *refs):
    lists = (refs[:pieces], refs[pieces : 2 * pieces])
    outs = refs[2 * pieces :]
    held, want, lent, me = plan[0], plan[3], plan[4], plan[5]
    for i in range(cap_units):
        home = i < held
        for src, group, dst in ((tok, lists[0], outs[0]), (cot, lists[1], outs[1])):
            start = MB_TOK + i * UNIT
            if not pieces:
                rows = src[start : start + UNIT, :]
                dst[i * UNIT : (i + 1) * UNIT, :] = jnp.where(home, rows, jnp.zeros_like(rows))
                continue
            width = group[0].shape[1]
            slots = group[0].shape[0] // UNIT
            place = want + i - held
            there = jnp.logical_and(jnp.logical_not(home), place < lent)
            at = pl.multiple_of(jnp.clip(place, 0, slots - 1) * UNIT, UNIT)
            for q in range(pieces):
                column = pl.multiple_of(jnp.bitwise_xor(me, q) * width, width)
                rows = src[start : start + UNIT, pl.ds(column, width)]
                guest = group[q][pl.ds(at, UNIT), :]
                rest = jnp.where(there, guest, jnp.zeros_like(guest))
                dst[i * UNIT : (i + 1) * UNIT, pl.ds(column, width)] = jnp.where(home, rows, rest)


def borrow(plan, tok, cot, tok_list, cot_list, cap_units):
    shape = jax.ShapeDtypeStruct((cap_units * UNIT, tok.shape[1]), jnp.bfloat16)
    pieces = len(tok_list)
    return pl.pallas_call(
        functools.partial(borrow_kernel, cap_units, pieces),
        out_shape=(shape, shape),
        in_specs=[SMEM] + [VMEM] * (2 + 2 * pieces),
        out_specs=(VMEM, VMEM),
        compiler_params=params(),
        cost_estimate=cost(0, tok.size * 4),
    )(plan, tok, cot, *tok_list, *cot_list)


def give_back_kernel(cap_units, slots, plan, half, out):
    held, want, lent = plan[0], plan[3], plan[4]
    owed = jnp.maximum(cap_units - held, 0)
    for j in range(slots):
        mine = jnp.logical_and(jnp.logical_and(j >= want, j < want + owed), j < lent)
        unit = jnp.clip(held + j - want, 0, cap_units - 1)
        rows = half[pl.ds(pl.multiple_of(MB_TOK + unit * UNIT, UNIT), UNIT), :]
        out[j * UNIT : (j + 1) * UNIT, :] = jnp.where(mine, rows, jnp.zeros_like(rows))


def give_back(plan, half, cap_units, slots):
    return pl.pallas_call(
        functools.partial(give_back_kernel, cap_units, slots),
        out_shape=jax.ShapeDtypeStruct((slots * UNIT, half.shape[1]), jnp.bfloat16),
        in_specs=[SMEM, VMEM],
        out_specs=VMEM,
        compiler_params=params(),
        cost_estimate=cost(0, half.size * 4),
    )(plan, half)


def settle_kernel(cap_units, slots, plan, half, *refs):
    out = refs[-1]
    held, first = plan[0], plan[2]
    out[:MB_TOK, :] = half[:MB_TOK, :]
    for i in range((out.shape[0] - MB_TOK) // UNIT):
        start = MB_TOK + i * UNIT
        if i < cap_units:
            rows = half[start : start + UNIT, :]
        else:
            at = pl.multiple_of(jnp.clip(first + i - cap_units, 0, slots - 1) * UNIT, UNIT)
            rows = refs[0][pl.ds(at, UNIT), :]
        out[start : start + UNIT, :] = jnp.where(i < held, rows, jnp.zeros_like(rows))


def settle(plan, half, returned, cap_units, slots, capacity):
    return pl.pallas_call(
        functools.partial(settle_kernel, cap_units, slots),
        out_shape=jax.ShapeDtypeStruct((capacity, half.shape[1]), jnp.bfloat16),
        in_specs=[SMEM] + [VMEM] * (1 + len(returned)),
        out_specs=VMEM,
        compiler_params=params(),
        cost_estimate=cost(0, half.size * 4),
    )(plan, half, *returned)


def join_kernel(pieces, plan, *refs):
    out = refs[-1]
    width = refs[0].shape[1]
    for q in range(pieces):
        column = pl.multiple_of(jnp.bitwise_xor(plan[5], q) * width, width)
        out[:, pl.ds(column, width)] = refs[q][...]


def join(plan, parts):
    rows, width = parts[0].shape
    return pl.pallas_call(
        functools.partial(join_kernel, len(parts)),
        out_shape=jax.ShapeDtypeStruct((rows, width * len(parts)), jnp.bfloat16),
        in_specs=[SMEM] + [VMEM] * len(parts),
        out_specs=VMEM,
        compiler_params=params(),
        cost_estimate=cost(0, rows * width * 8),
    )(plan, *parts)


def spread_over_dp(x, order):
    for bit in order:
        x = x + swap(x, "dp", bit)
    return x


def over_row(x):
    return [x] + [swap(x, "row", q) for q in range(1, lax.axis_size("row"))]


def most_lent(size, cap_units):
    per_mb = MB_TOK // UNIT
    best = {0: 0}
    for _ in range(size):
        step = {}
        for total, lent in best.items():
            for extra in range(0, MB_MAX * per_mb, per_mb):
                key = total + extra
                if key <= size * cap_units:
                    step[key] = max(step.get(key, 0), lent + max(extra - cap_units, 0))
        best = step
    return max(best.values())


def sum_inward(far, near):
    far_in = lax.ppermute(far, "col", INWARD)
    near_in = lax.ppermute(near, "col", INWARD)
    crossing = (far.astype(jnp.float32) + far_in.astype(jnp.float32)).astype(jnp.bfloat16)
    across = lax.ppermute(crossing, "col", MIDDLE)
    return (
        near.astype(jnp.float32) + near_in.astype(jnp.float32) + across.astype(jnp.float32)
    )


def send_outward(near, inner):
    far = lax.ppermute(near, "col", MIDDLE)
    near_out = lax.ppermute(near, "col", OUTWARD)
    far_out = lax.ppermute(far, "col", OUTWARD)
    return jnp.concatenate(
        [jnp.where(inner, far, far_out), jnp.where(inner, near, near_out)], axis=0
    )


def branch(cap_units, capacity, th, tw, args):
    (meta, plan, total, first_hidden, first_act, tokens, cotangent, up_tile, up_from, up_into,
     down_tile, down_from, down_into) = args
    size = lax.axis_size("dp")
    row_size = lax.axis_size("row")
    bits = bits_of(size)
    other = bits[1:] + bits[:1]
    inner = jnp.logical_or(lax.axis_index("col") == 1, lax.axis_index("col") == 2)
    slots = most_lent(size, cap_units)

    tok_list, cot_list = [], []
    if slots:
        tok_lent, cot_lent = lend(plan, tokens, cotangent, cap_units, slots, row_size)
        tok_list = over_row(spread_over_dp(tok_lent, bits))
        cot_list = over_row(spread_over_dp(cot_lent, other))
    tok_extra, cot_extra = borrow(plan, tokens, cotangent, tok_list, cot_list, cap_units)
    toks = [tokens[:MB_TOK], tok_extra]
    cots = [cotangent[:MB_TOK], cot_extra]

    parts = [first_hidden, spread(meta, tok_extra, up_tile, up_from, up_into, th, False)]
    sums = [sum_inward(*p) for p in parts]
    acts = [send_outward(gelu_exact(h).astype(jnp.bfloat16), inner) for h in sums]

    back = [first_act, spread(meta, cot_extra, down_tile, down_into, down_from, th, True)]
    slopes = [gelu_slope(h) for h in sums]
    hgrads = [
        send_outward((sum_inward(*b) * s).astype(jnp.bfloat16), inner)
        for b, s in zip(back, slopes, strict=True)
    ]

    def finish(pieces):
        half = pieces[0].astype(jnp.float32)
        for q in range(1, row_size):
            half = half + swap(pieces[q], "row", q).astype(jnp.float32)
        half = half.astype(jnp.bfloat16)
        returned = []
        if slots:
            sent = give_back(plan, half, cap_units, slots)
            returned = [spread_over_dp(sent, bits)]
        mine = settle(plan, half, returned, cap_units, slots, capacity)
        return join(plan, over_row(mine))

    y_out = finish(collect(meta, acts, down_tile, down_from, down_into, tw, row_size, False))
    grad_down = reduce_grads(meta, acts, cots, True, down_from, down_into, total, size, th)
    grad_tokens = finish(collect(meta, hgrads, up_tile, up_into, up_from, tw, row_size, True))
    grad_up = reduce_grads(meta, toks, hgrads, False, up_from, up_into, total, size, th)
    return (y_out, grad_tokens, grad_up, grad_down)


def body(tokens, cotangent, counts, up_blocks, up_rows, up_cols, down_blocks, down_rows, down_cols):
    capacity = tokens.shape[0]
    block = up_blocks.shape[-1]
    tw = tokens.shape[1] // block
    th = FF // lax.axis_size("row") // block
    size = lax.axis_size("dp")
    me = lax.axis_index("dp")
    up_tile, up_from, up_into = up_blocks[0, 0], up_rows[0, 0], up_cols[0, 0]
    down_tile, down_from, down_into = down_blocks[0, 0], down_rows[0, 0], down_cols[0, 0]
    side = (lax.axis_index("col") >= 2).astype(jnp.int32)
    row = lax.axis_index("row")
    meta = jnp.stack([side, row, me]).astype(jnp.int32)

    places = jnp.arange(size, dtype=jnp.int32)
    every = jnp.where(places == me, counts[0], 0)
    for bit in bits_of(size):
        every = every + swap(every, "dp", bit)

    first_hidden = spread(meta, tokens[:MB_TOK], up_tile, up_from, up_into, th, False)
    first_act = spread(meta, cotangent[:MB_TOK], down_tile, down_into, down_from, th, True)

    count = jnp.sum(every)
    total = count.astype(jnp.float32)[None]
    held = (every - 1) * (MB_TOK // UNIT)
    needed = (jnp.sum(held) + size - 1) // size
    options = [c for c in CAPACITIES if c * UNIT <= capacity - MB_TOK]
    pick = jnp.sum((needed > jnp.array(options[:-1], jnp.int32)).astype(jnp.int32))

    def one(cap_units, args):
        held, *rest = args
        spare = jnp.maximum(held - cap_units, 0)
        want = jnp.maximum(cap_units - held, 0)
        before = places < me
        at_me = places == me

        def pick_sum(mask, values):
            return jnp.sum(jnp.where(mask, values, 0))

        plan = jnp.stack(
            [
                pick_sum(at_me, held),
                pick_sum(at_me, spare),
                pick_sum(before, spare),
                pick_sum(before, want),
                jnp.sum(spare),
                row,
            ]
        ).astype(jnp.int32)
        return branch(cap_units, capacity, th, tw, (rest[0], plan, *rest[1:]))

    y_out, grad_tokens, grad_up, grad_down = lax.switch(
        pick,
        [functools.partial(one, c) for c in options],
        (held, meta, total, first_hidden, first_act, tokens, cotangent, up_tile, up_from, up_into,
         down_tile, down_from, down_into),
    )
    return (y_out, grad_tokens, grad_up[None, None], grad_down[None, None])


def solution(mesh):
    return jax.shard_map(
        body,
        mesh=mesh,
        in_specs=(
            P("dp", "col"),
            P("dp", "col"),
            P("dp"),
            P("col", "row", None, None, None),
            P("col", "row", None),
            P("col", "row", None),
            P("row", "col", None, None, None),
            P("row", "col", None),
            P("row", "col", None),
        ),
        out_specs=(
            P("dp", "col"),
            P("dp", "col"),
            P("col", "row", "dp", None, None),
            P("row", "col", "dp", None, None),
        ),
        check_vma=False,
    )
```

```python
import functools

import jax
import jax.numpy as jnp
from jax import lax
from jax.experimental import pallas as pl
from jax.experimental.pallas import tpu as pltpu
from jax.sharding import PartitionSpec as P

FF = 16384
MB_TOK = 64
MB_MAX = 4
UNIT = 16
PER_MB = MB_TOK // UNIT
SPARE = (MB_MAX - 1) * PER_MB
BATCH = 8
GROUP = 64
VMEM_LIMIT = 48 * 1024 * 1024
CAPACITIES = (3, 6, 12)
GATHER_MOST = 4

SMEM = pl.BlockSpec(memory_space=pltpu.SMEM)
VMEM = pl.BlockSpec(memory_space=pltpu.VMEM)

INWARD = [(0, 1), (3, 2)]
MIDDLE = [(1, 2), (2, 1)]
OUTWARD = [(1, 0), (2, 3)]


def gelu_exact(hidden_in):
    return 0.5 * hidden_in * (1.0 + lax.erf(hidden_in * 0.7071067811865476))


def gelu_slope(hidden_in):
    normal_cdf = 0.5 * (1.0 + lax.erf(hidden_in * 0.7071067811865476))
    return normal_cdf + hidden_in * jnp.exp(-0.5 * hidden_in * hidden_in) * 0.3989422804014327


def swap(x, axis, mask):
    size = lax.axis_size(axis)
    return lax.ppermute(x, axis, [(i, i ^ mask) for i in range(size)])


def along(x, pairs):
    return lax.ppermute(x, "col", pairs)


def tie(x, *after):
    return lax.optimization_barrier((x, *after))[0]


def params():
    return pltpu.CompilerParams(vmem_limit_bytes=VMEM_LIMIT)


def cost(flops, moved):
    return pl.CostEstimate(flops=flops, bytes_accessed=moved, transcendentals=0)


def cost_us(time):
    return cost(int(time * 1.1e9), 0)


def slot_of(index, side, count):
    moved = index + side * (count // 2)
    return jnp.where(moved >= count, moved - count, moved)


def lanes(ref, index, block):
    return ref[:, pl.ds(pl.multiple_of(index * block, block), block)]


def unit_rows(ref, unit, start=0):
    return ref[pl.ds(pl.multiple_of(start + unit * UNIT, UNIT), UNIT), :]


def block_dot(a, w, flipped):
    return lax.dot_general(
        a, w, (((1,), (1 if flipped else 0,)), ((), ())), preferred_element_type=jnp.float32
    )


def spread_kernel(th, group, flipped, meta, take, put, x_ref, w_ref, far_ref, near_ref, acc):
    g = pl.program_id(0)
    block = w_ref.shape[-1]
    half = th // 2
    side = meta[0]

    @pl.when(g == 0)
    def _():
        @pl.loop(0, acc.shape[0])
        def _(i):
            acc[i] = jnp.zeros(acc.shape[1:], jnp.float32)

    step = min(BATCH, group)

    def run(s, carry):
        products = []
        for j in range(step):
            a = lanes(x_ref, take[g * group + s * step + j], block)
            products.append(block_dot(a, w_ref[s * step + j], flipped))
        for j in range(step):
            o = slot_of(put[g * group + s * step + j], side, th)
            acc[o] += products[j]
        return carry

    lax.fori_loop(0, group // step, run, 0)

    @pl.when(g == pl.num_programs(0) - 1)
    def _():
        @pl.loop(0, half)
        def _(i):
            far_ref[i] = acc[i].astype(jnp.bfloat16)
            near_ref[i] = acc[half + i].astype(jnp.bfloat16)


def spread(meta, x, place, rows, width, blocks, take, put, th, flipped):
    nb, block, _ = blocks.shape
    group = min(GROUP, nb)
    shape = jax.ShapeDtypeStruct((th // 2, rows, block), jnp.bfloat16)
    whole = pl.BlockSpec((th // 2, rows, block), lambda g, *_: (0, 0, 0))
    return pl.pallas_call(
        functools.partial(spread_kernel, th, group, flipped),
        out_shape=(shape, shape),
        grid_spec=pltpu.PrefetchScalarGridSpec(
            num_scalar_prefetch=3,
            grid=(nb // group,),
            in_specs=[
                pl.BlockSpec((rows, width), lambda g, *_: place),
                pl.BlockSpec((group, block, block), lambda g, *_: (g, 0, 0)),
            ],
            out_specs=(whole, whole),
            scratch_shapes=[pltpu.VMEM((th, rows, block), jnp.float32)],
        ),
        compiler_params=params(),
        cost_estimate=cost_us(10),
    )(meta, take, put, x, blocks)


def collect_kernel(th, group, flipped, parts, meta, take, put, *refs):
    h_refs = refs[:parts]
    w_ref, out_ref, acc = refs[parts:]
    g = pl.program_id(0)
    side = meta[0]
    block = w_ref.shape[-1]

    @pl.when(g == 0)
    def _():
        @pl.loop(0, acc.shape[0])
        def _(i):
            acc[i] = jnp.zeros(acc.shape[1:], jnp.float32)

    step = min(BATCH, group)

    def run(s, carry):
        products = []
        for j in range(step):
            i = slot_of(take[g * group + s * step + j], side, th)
            a = jnp.concatenate([h[i] for h in h_refs], axis=0)
            products.append(block_dot(a, w_ref[s * step + j], flipped))
        for j in range(step):
            acc[put[g * group + s * step + j]] += products[j]
        return carry

    lax.fori_loop(0, group // step, run, 0)

    @pl.when(g == pl.num_programs(0) - 1)
    def _():
        for t in range(acc.shape[0]):
            out_ref[:, t * block : (t + 1) * block] = acc[t].astype(jnp.bfloat16)


def collect(meta, hs, blocks, take, put, tw, flipped):
    th, _, block = hs[0].shape
    rows = sum(h.shape[1] for h in hs)
    nb = blocks.shape[0]
    group = min(GROUP, nb)
    return pl.pallas_call(
        functools.partial(collect_kernel, th, group, flipped, len(hs)),
        out_shape=jax.ShapeDtypeStruct((rows, tw * block), jnp.bfloat16),
        grid_spec=pltpu.PrefetchScalarGridSpec(
            num_scalar_prefetch=3,
            grid=(nb // group,),
            in_specs=[pl.BlockSpec(h.shape, lambda g, *_: (0, 0, 0)) for h in hs]
            + [pl.BlockSpec((group, block, block), lambda g, *_: (g, 0, 0))],
            out_specs=pl.BlockSpec((rows, tw * block), lambda g, *_: (0, 0)),
            scratch_shapes=[pltpu.VMEM((tw, rows, block), jnp.float32)],
        ),
        compiler_params=params(),
        cost_estimate=cost_us(30),
    )(meta, take, put, *hs, blocks)


def pack_kernel(size, meta, index, far_mid, far_out, near_own, near_out, full, *chosen):
    side, me, inner = meta[0], meta[2], meta[3]
    th = full.shape[0]
    half = th // 2

    @pl.when(inner == 1)
    def _():
        @pl.loop(0, half)
        def _(i):
            full[i] = far_mid[i]
            full[half + i] = near_own[i]

    @pl.when(inner == 0)
    def _():
        @pl.loop(0, half)
        def _(i):
            full[i] = far_out[i]
            full[half + i] = near_out[i]

    if size > 1:
        share = chosen[0].shape[0]
        step = min(4, share)

        @pl.loop(0, share // step)
        def _(b):
            for mask in range(1, size):
                base = jnp.bitwise_xor(me, mask) * share
                for j in range(step):
                    i = b * step + j
                    chosen[mask - 1][i] = full[slot_of(index[base + i], side, th)]


def pack(meta, index, far_mid, far_out, near_own, near_out, size):
    half, rows, block = near_own.shape
    share = index.shape[0] // size
    chosen = jax.ShapeDtypeStruct((share, rows, block), jnp.bfloat16)
    out = pl.pallas_call(
        functools.partial(pack_kernel, size),
        out_shape=(jax.ShapeDtypeStruct((2 * half, rows, block), jnp.bfloat16),)
        + (chosen,) * (size - 1),
        in_specs=[SMEM] * 2 + [VMEM] * 4,
        out_specs=(VMEM,) * size,
        compiler_params=params(),
        cost_estimate=cost(0, half * rows * block * 16),
    )(meta, index, far_mid, far_out, near_own, near_out)
    return out[0], out[1:]


def grads_kernel(th, chunks, widths, size, hidden_left, offset, meta, hid, wid, total, *refs):
    out = refs[-1]
    share, block, _ = out.shape
    side, me = meta[0], meta[2]
    hidden = [refs[m * chunks : (m + 1) * chunks] for m in range(size)]
    base = size * chunks
    width = [refs[base + m * widths : base + (m + 1) * widths] for m in range(size)]
    step = min(2, share)

    def run(b, carry):
        products = []
        for j in range(step):
            i = b * step + j
            k = me * share + i
            own = slot_of(hid[k], side, th)
            h = jnp.concatenate(
                [r[own if m == 0 else i] for m in range(size) for r in hidden[m]], axis=0
            )
            w = jnp.concatenate(
                [lanes(r, wid[k] + offset, block) for m in range(size) for r in width[m]], axis=0
            )
            a, c = (h, w) if hidden_left else (w, h)
            products.append(
                lax.dot_general(a, c, (((0,), (0,)), ((), ())), preferred_element_type=jnp.float32)
            )
        for j in range(step):
            out[b * step + j] = products[j] / total[0]
        return carry

    lax.fori_loop(0, share // step, run, 0)


def grads(meta, hidden, width, hidden_left, offset, hid, wid, total, size, th):
    block = hidden[0][0].shape[-1]
    share = hid.shape[0] // size
    rows = sum(w.shape[0] for w in width[0])
    flat = [r for group in hidden for r in group] + [r for group in width for r in group]
    return pl.pallas_call(
        functools.partial(
            grads_kernel, th, len(hidden[0]), len(width[0]), size, hidden_left, offset
        ),
        out_shape=jax.ShapeDtypeStruct((share, block, block), jnp.float32),
        in_specs=[SMEM] * 4 + [VMEM] * len(flat),
        out_specs=VMEM,
        compiler_params=params(),
        cost_estimate=cost_us(30),
    )(meta, hid, wid, total, *flat)


def prefix(values, d):
    return sum(jnp.where(e < d, v, 0) for e, v in enumerate(values))


def entry(values, d):
    return sum(jnp.where(e == d, v, 0) for e, v in enumerate(values))


class Plan:
    def __init__(self, every, cap):
        held = [(every[d] - 1) * PER_MB for d in range(every.shape[0])]
        self.held = held
        self.spare = [jnp.maximum(h - cap, 0) for h in held]
        self.owed = [jnp.maximum(cap - h, 0) for h in held]

    def span(self, lender, borrower):
        first, want = prefix(self.spare, lender), prefix(self.owed, borrower)
        low = jnp.maximum(first, want)
        high = jnp.minimum(first + entry(self.spare, lender), want + entry(self.owed, borrower))
        return low, high, first, want


def options_for(capacity):
    return [c for c in CAPACITIES if c * UNIT <= capacity - MB_TOK]


def most_lent(cap):
    return min(cap, SPARE - cap)


def lend_kernel(options, every, meta, tok, cot, *outs):
    size = every.shape[0]
    row, me = meta[1], meta[2]
    needed = (sum((every[d] - 1) * PER_MB for d in range(size)) + size - 1) // size
    cap = options[0]
    for small, large in zip(options[:-1], options[1:], strict=True):
        cap = cap + jnp.where(needed > small, large - small, 0)
    plan = Plan(every, cap)
    width = outs[0].shape[1] // 2
    column = pl.multiple_of(row * width, width)
    for mask in range(1, size):
        low, _, first, _ = plan.span(me, jnp.bitwise_xor(me, mask))
        out = outs[mask - 1]

        @pl.loop(0, out.shape[0] // UNIT)
        def _(s, out=out, low=low, first=first):
            unit = jnp.clip(cap + low + s - first, 0, SPARE - 1)
            rows = pl.ds(pl.multiple_of(MB_TOK + unit * UNIT, UNIT), UNIT)
            here = pl.ds(pl.multiple_of(s * UNIT, UNIT), UNIT)
            out[here, :width] = tok[rows, pl.ds(column, width)]
            out[here, width:] = cot[rows, pl.ds(column, width)]


def lend(every, meta, tok, cot, options, size, pieces):
    slots = max(most_lent(c) for c in options)
    shape = jax.ShapeDtypeStruct((slots * UNIT, 2 * tok.shape[1] // pieces), jnp.bfloat16)
    return pl.pallas_call(
        functools.partial(lend_kernel, options),
        out_shape=(shape,) * (size - 1),
        in_specs=[SMEM, SMEM, VMEM, VMEM],
        out_specs=(VMEM,) * (size - 1),
        compiler_params=params(),
        cost_estimate=cost(0, tok.size * 4),
    )(every, meta, tok, cot)


def borrow_kernel(cap, pieces, every, meta, tok, cot, *refs):
    out = refs[-1]
    lists = refs[:-1]
    row, me = meta[1], meta[2]
    plan = Plan(every, cap)
    held = entry(plan.held, me)
    whole = tok.shape[1]
    @pl.loop(0, cap)
    def _(i):
        here = pl.ds(pl.multiple_of(i * UNIT, UNIT), UNIT)
        there = pl.ds(pl.multiple_of(MB_TOK + i * UNIT, UNIT), UNIT)

        @pl.when(i < held)
        def _():
            out[here, :whole] = tok[there, :]
            out[here, whole:] = cot[there, :]

        @pl.when(i >= held)
        def _():
            out[here, :] = jnp.zeros((UNIT, 2 * whole), jnp.bfloat16)

    for n in range(len(lists) // pieces):
        low, high, _, want = plan.span(jnp.bitwise_xor(me, n + 1), me)
        width = lists[0].shape[1] // 2

        @pl.loop(0, cap)
        def _(i, n=n, low=low, high=high, want=want):
            at = want + i - held
            there = jnp.logical_and(i >= held, jnp.logical_and(at >= low, at < high))

            @pl.when(there)
            def _():
                rows = pl.ds(pl.multiple_of((at - low) * UNIT, UNIT), UNIT)
                here = pl.ds(pl.multiple_of(i * UNIT, UNIT), UNIT)
                for q in range(pieces):
                    column = pl.multiple_of(jnp.bitwise_xor(row, q) * width, width)
                    guest = lists[n * pieces + q]
                    out[here, pl.ds(column, width)] = guest[rows, :width]
                    out[here, pl.ds(column + whole, width)] = guest[rows, width:]


def borrow(every, meta, tok, cot, lists, cap, pieces):
    flat = [r for group in lists for r in group] if most_lent(cap) else []
    return pl.pallas_call(
        functools.partial(borrow_kernel, cap, pieces),
        out_shape=jax.ShapeDtypeStruct((cap * UNIT, 2 * tok.shape[1]), jnp.bfloat16),
        in_specs=[SMEM, SMEM] + [VMEM] * (2 + len(flat)),
        out_specs=VMEM,
        compiler_params=params(),
        cost_estimate=cost(0, tok.size * 4),
    )(every, meta, tok, cot, *flat)


def give_back_kernel(cap, every, meta, done, *outs):
    me = meta[2]
    plan = Plan(every, cap)
    held = entry(plan.held, me)
    for n, out in enumerate(outs):
        low, _, _, want = plan.span(jnp.bitwise_xor(me, n + 1), me)

        @pl.loop(0, out.shape[0] // UNIT)
        def _(s, out=out, low=low, want=want):
            unit = jnp.clip(held + low + s - want, 0, cap - 1)
            out[pl.ds(pl.multiple_of(s * UNIT, UNIT), UNIT), :] = unit_rows(done, unit)


def give_back(every, meta, done, cap, size):
    shape = jax.ShapeDtypeStruct((most_lent(cap) * UNIT, done.shape[1]), jnp.bfloat16)
    return pl.pallas_call(
        functools.partial(give_back_kernel, cap),
        out_shape=(shape,) * (size - 1),
        in_specs=[SMEM, SMEM, VMEM],
        out_specs=(VMEM,) * (size - 1),
        compiler_params=params(),
        cost_estimate=cost(0, done.size * 4),
    )(every, meta, done)


def settle_kernel(cap, every, meta, first_mb, extra, *refs):
    out = refs[-1]
    me = meta[2]
    plan = Plan(every, cap)
    held = entry(plan.held, me)
    width = out.shape[1]

    @pl.loop(0, PER_MB)
    def _(i):
        here = pl.ds(pl.multiple_of(i * UNIT, UNIT), UNIT)
        out[here, :] = first_mb[here, :]

    @pl.loop(0, (out.shape[0] - MB_TOK) // UNIT)
    def _(i):
        here = pl.ds(pl.multiple_of(MB_TOK + i * UNIT, UNIT), UNIT)
        own = jnp.logical_and(i < cap, i < held)

        @pl.when(own)
        def _():
            out[here, :] = unit_rows(extra, i)

        @pl.when(jnp.logical_not(own))
        def _():
            out[here, :] = jnp.zeros((UNIT, width), jnp.bfloat16)

    for n, guest in enumerate(refs[:-1]):
        low, high, first, _ = plan.span(me, jnp.bitwise_xor(me, n + 1))

        @pl.loop(cap, (out.shape[0] - MB_TOK) // UNIT)
        def _(i, guest=guest, low=low, high=high, first=first):
            at = first + i - cap
            there = jnp.logical_and(i < held, jnp.logical_and(at >= low, at < high))

            @pl.when(there)
            def _():
                here = pl.ds(pl.multiple_of(MB_TOK + i * UNIT, UNIT), UNIT)
                out[here, :] = unit_rows(guest, at - low)


def settle(every, meta, first_mb, extra, returned, cap, capacity):
    return pl.pallas_call(
        functools.partial(settle_kernel, cap),
        out_shape=jax.ShapeDtypeStruct((capacity, extra.shape[1]), jnp.bfloat16),
        in_specs=[SMEM, SMEM] + [VMEM] * (2 + len(returned)),
        out_specs=VMEM,
        compiler_params=params(),
        cost_estimate=cost(0, extra.size * 4),
    )(every, meta, first_mb, extra, *returned)


def over_row(x):
    return [x] + [swap(x, "row", q) for q in range(1, lax.axis_size("row"))]


def add_over_row(x):
    if lax.axis_size("row") == 2:
        return (x.astype(jnp.float32) + swap(x, "row", 1).astype(jnp.float32)).astype(x.dtype)
    return lax.psum(x.astype(jnp.float32), "row").astype(x.dtype)


def over_dp(x):
    return [swap(x, "dp", mask) for mask in range(1, lax.axis_size("dp"))]


def plus(*terms):
    return sum(t.astype(jnp.float32) for t in terms)


def branch(cap, capacity, th, tw, args):
    (every, meta, total, first, first_back, first_lists, first_rows, tokens, cotangent, up_tile,
     up_from, up_into, down_tile, down_from, down_into) = args
    size = lax.axis_size("dp")
    gather = size <= GATHER_MOST
    parts = size if gather else 1
    width = tokens.shape[1]
    pieces = lax.axis_size("row")
    rows = cap * UNIT

    def to_owners(chosen):
        return [swap(x, "dp", m + 1) for m, x in enumerate(chosen)]

    def to_all(x):
        return [swap(x, "dp", m) for m in range(1, size)] if gather else []

    def crossing(far, far_in):
        return along(plus(far, far_in).astype(jnp.bfloat16), MIDDLE)

    a_far, a_near = first_back
    a_sum = plus(*first)
    a_act = gelu_exact(a_sum).astype(jnp.bfloat16)
    a_far_in = along(a_far, INWARD)
    a_act_mid = along(a_act, MIDDLE)
    a_act_near = along(a_act, OUTWARD)

    extra = borrow(every, meta, tokens, cotangent, first_lists, cap, pieces)
    b_far, b_near = spread(
        meta, extra, (0, 0), rows, width, up_tile, up_from, up_into, th, False
    )
    b_far_in = along(b_far, INWARD)
    b_back_far, b_back_near = spread(
        meta, extra, (0, 1), rows, width, down_tile, down_into, down_from, th, True
    )

    a_act_far = along(a_act_mid, OUTWARD)
    a_near_in = along(tie(a_near, a_far_in, a_act_mid, b_far), INWARD)
    a_across = crossing(a_far, a_far_in)

    b_near_in = along(tie(b_near, b_far_in, a_act_far, b_back_far), INWARD)
    b_across = crossing(b_far, b_far_in)

    a_full, a_chosen = pack(meta, down_from, a_act_mid, a_act_far, a_act, a_act_near, parts)
    live = jnp.concatenate([first_rows, extra], axis=0)
    live_got = to_all(live)

    a_slope = gelu_slope(a_sum)
    a_grad = plus(a_near, a_near_in, tie(a_across, b_far_in, *a_chosen))
    a_grad = (a_grad * a_slope).astype(jnp.bfloat16)
    a_grad_mid = along(a_grad, MIDDLE)
    a_grad_near = along(a_grad, OUTWARD)

    b_sum = plus(b_near, b_near_in, tie(b_across, *live_got))
    b_act = gelu_exact(b_sum).astype(jnp.bfloat16)
    b_act_mid = along(b_act, MIDDLE)
    b_act_near = along(b_act, OUTWARD)
    b_back_far_in = along(tie(b_back_far, b_near_in, b_across), INWARD)
    a_got = to_owners(a_chosen)

    a_grad_far = along(tie(a_grad_mid, b_back_far_in), OUTWARD)

    b_act_far = along(tie(b_act_mid, a_grad_near), OUTWARD)
    b_back_near_in = along(tie(b_back_near, b_back_far_in, *a_got), INWARD)
    b_back_across = crossing(b_back_far, b_back_far_in)

    a_hgrad, a_hchosen = pack(
        meta, up_into, a_grad_mid, a_grad_far, a_grad, a_grad_near, parts
    )
    b_grad = plus(b_back_near, b_back_near_in, tie(b_back_across, *a_hchosen))
    b_grad = (b_grad * gelu_slope(b_sum)).astype(jnp.bfloat16)
    b_grad_mid = along(b_grad, MIDDLE)
    b_grad_near = along(b_grad, OUTWARD)
    a_hgot = to_owners(a_hchosen)

    b_full, b_chosen = pack(meta, down_from, b_act_mid, b_act_far, b_act, b_act_near, parts)
    b_grad_far = along(tie(b_grad_mid, *b_chosen, *a_hgot), OUTWARD)
    b_got = to_owners(b_chosen)
    b_hgrad, b_hchosen = pack(
        meta, up_into, b_grad_mid, b_grad_far, b_grad, b_grad_near, parts
    )
    b_hgot = to_owners(b_hchosen)

    def finish(a, b, blocks, take, put, flipped, after):
        first_mb = add_over_row(collect(meta, [a], blocks, take, put, tw, flipped))
        rest = add_over_row(collect(meta, [b], blocks, take, put, tw, flipped))
        returned = []
        if most_lent(cap):
            sent = give_back(every, meta, tie(rest, *after) if after else rest, cap, size)
            returned = to_owners(sent)
        return settle(every, meta, first_mb, rest, returned, cap, capacity)

    rows_of = [[x] for x in [live] + live_got]

    def owned(a, b, a_got, b_got, hidden_left, offset, hid, wid):
        hidden = [[a, b]] + [list(g) for g in zip(a_got, b_got, strict=True)]
        if gather:
            return grads(meta, hidden, rows_of, hidden_left, offset, hid, wid, total, size, th)
        mine = grads(
            meta * jnp.array([1, 1, 0, 1], jnp.int32), hidden, rows_of, hidden_left, offset, hid,
            wid, jnp.ones_like(total), 1, th,
        )
        share = lax.psum_scatter(
            mine.astype(jnp.bfloat16), "dp", scatter_dimension=0, tiled=True
        )
        return share.astype(jnp.float32) / total[0]

    y_out = finish(a_full, b_full, down_tile, down_from, down_into, False, ())
    grad_down = owned(a_full, b_full, a_got, b_got, True, tw, down_from, down_into)
    grad_tokens = finish(a_hgrad, b_hgrad, up_tile, up_into, up_from, True, b_hgot)
    grad_up = owned(a_hgrad, b_hgrad, a_hgot, b_hgot, False, 0, up_into, up_from)
    return (y_out, grad_tokens, grad_up, grad_down)


def body(tokens, cotangent, counts, up_blocks, up_rows, up_cols, down_blocks, down_rows, down_cols):
    capacity, width = tokens.shape
    block = up_blocks.shape[-1]
    tw = width // block
    th = FF // lax.axis_size("row") // block
    size = lax.axis_size("dp")
    me = lax.axis_index("dp")
    up_tile, up_from, up_into = up_blocks[0, 0], up_rows[0, 0], up_cols[0, 0]
    down_tile, down_from, down_into = down_blocks[0, 0], down_rows[0, 0], down_cols[0, 0]
    col = lax.axis_index("col")
    inner = jnp.logical_or(col == 1, col == 2)
    meta = jnp.stack([col >= 2, lax.axis_index("row"), me, inner]).astype(jnp.int32)

    places = jnp.arange(size, dtype=jnp.int32)
    every = jnp.where(places == me, counts[0], 0)
    far, near = spread(meta, tokens, (0, 0), MB_TOK, width, up_tile, up_from, up_into, th, False)
    for bit in range(size.bit_length() - 1):
        every = every + swap(every if bit == 0 else tie(every, far), "dp", 1 << bit)

    far_in = along(far, INWARD)
    near_in = along(near, INWARD)
    across = along(plus(far, far_in).astype(jnp.bfloat16), MIDDLE)
    first_back = spread(
        meta, cotangent, (0, 0), MB_TOK, width, down_tile, down_into, down_from, th, True
    )

    options = options_for(capacity)
    lent = lend(tie(every, *first_back), meta, tokens, cotangent, options, size, lax.axis_size("row"))
    lists = [over_row(swap(x, "dp", m + 1)) for m, x in enumerate(lent)]
    first_rows = jnp.concatenate([tokens[:MB_TOK], cotangent[:MB_TOK]], axis=1)

    total = jnp.sum(every).astype(jnp.float32)[None]
    needed = (jnp.sum(every - 1) * PER_MB + size - 1) // size
    args = (every, meta, total, (near, near_in, across), first_back, lists, first_rows, tokens,
            cotangent, up_tile, up_from, up_into, down_tile, down_from, down_into)

    def choose(group, args):
        if len(group) == 1:
            return branch(group[0], capacity, th, tw, args)
        middle = len(group) // 2
        return lax.cond(
            needed > group[middle - 1],
            functools.partial(choose, group[middle:]),
            functools.partial(choose, group[:middle]),
            args,
        )

    y_out, grad_tokens, grad_up, grad_down = choose(options, args)
    return (y_out, grad_tokens, grad_up[None, None], grad_down[None, None])


def solution(mesh):
    return jax.shard_map(
        body,
        mesh=mesh,
        in_specs=(
            P("dp", "col"),
            P("dp", "col"),
            P("dp"),
            P("col", "row", None, None, None),
            P("col", "row", None),
            P("col", "row", None),
            P("row", "col", None, None, None),
            P("row", "col", None),
            P("row", "col", None),
        ),
        out_specs=(
            P("dp", "col"),
            P("dp", "col"),
            P("col", "row", "dp", None, None),
            P("row", "col", "dp", None, None),
        ),
        check_vma=False,
    )
```

```python
import functools

import jax
import jax.numpy as jnp
from jax import lax
from jax.experimental import pallas as pl
from jax.experimental.pallas import tpu as pltpu
from jax.sharding import PartitionSpec as P

FF = 16384
MB_TOK = 64
MB_MAX = 4
UNIT = 16
PER_MB = MB_TOK // UNIT
SPARE = (MB_MAX - 1) * PER_MB
BATCH = 8
GROUP = 64
VMEM_BASE = 8 * 1024 * 1024
VMEM_ROW = 64 * 1024
CAPACITIES = (3, 6, 12)
GATHER_MOST = 4

SMEM = pl.BlockSpec(memory_space=pltpu.SMEM)
VMEM = pl.BlockSpec(memory_space=pltpu.VMEM)

INWARD = [(0, 1), (3, 2)]
MIDDLE = [(1, 2), (2, 1)]
OUTWARD = [(1, 0), (2, 3)]


def gelu_exact(hidden_in):
    return 0.5 * hidden_in * (1.0 + lax.erf(hidden_in * 0.7071067811865476))


def gelu_slope(hidden_in):
    normal_cdf = 0.5 * (1.0 + lax.erf(hidden_in * 0.7071067811865476))
    return normal_cdf + hidden_in * jnp.exp(-0.5 * hidden_in * hidden_in) * 0.3989422804014327


def swap(x, axis, mask):
    size = lax.axis_size(axis)
    return lax.ppermute(x, axis, [(i, i ^ mask) for i in range(size)])


def along(x, pairs):
    return lax.ppermute(x, "col", pairs)


def tie(x, *after):
    return lax.optimization_barrier((x, *after))[0]


def params(rows=64):
    return pltpu.CompilerParams(vmem_limit_bytes=VMEM_BASE + rows * VMEM_ROW)


def cost(flops, moved):
    return pl.CostEstimate(flops=flops, bytes_accessed=moved, transcendentals=0)


def cost_us(time):
    return cost(int(time * 1.1e9), 0)


def slot_of(index, side, count):
    moved = index + side * (count // 2)
    return jnp.where(moved >= count, moved - count, moved)


def lanes(ref, index, block):
    return ref[:, pl.ds(pl.multiple_of(index * block, block), block)]


def unit_rows(ref, unit, start=0):
    return ref[pl.ds(pl.multiple_of(start + unit * UNIT, UNIT), UNIT), :]


def block_dot(a, w, flipped):
    return lax.dot_general(
        a, w, (((1,), (1 if flipped else 0,)), ((), ())), preferred_element_type=jnp.float32
    )


def spread_kernel(th, group, flipped, meta, take, put, x_ref, w_ref, far_ref, near_ref, acc):
    g = pl.program_id(0)
    block = w_ref.shape[-1]
    half = th // 2
    side = meta[0]

    @pl.when(g == 0)
    def _():
        @pl.loop(0, acc.shape[0])
        def _(i):
            acc[i] = jnp.zeros(acc.shape[1:], jnp.float32)

    step = min(BATCH, group)

    def run(s, carry):
        products = []
        for j in range(step):
            a = lanes(x_ref, take[g * group + s * step + j], block)
            products.append(block_dot(a, w_ref[s * step + j], flipped))
        for j in range(step):
            o = slot_of(put[g * group + s * step + j], side, th)
            acc[o] += products[j]
        return carry

    lax.fori_loop(0, group // step, run, 0)

    @pl.when(g == pl.num_programs(0) - 1)
    def _():
        @pl.loop(0, half)
        def _(i):
            far_ref[i] = acc[i].astype(jnp.bfloat16)
            near_ref[i] = acc[half + i].astype(jnp.bfloat16)


def spread(meta, x, place, rows, width, blocks, take, put, th, flipped):
    nb, block, _ = blocks.shape
    group = min(GROUP, nb)
    shape = jax.ShapeDtypeStruct((th // 2, rows, block), jnp.bfloat16)
    whole = pl.BlockSpec((th // 2, rows, block), lambda g, *_: (0, 0, 0))
    return pl.pallas_call(
        functools.partial(spread_kernel, th, group, flipped),
        out_shape=(shape, shape),
        grid_spec=pltpu.PrefetchScalarGridSpec(
            num_scalar_prefetch=3,
            grid=(nb // group,),
            in_specs=[
                pl.BlockSpec((rows, width), lambda g, *_: place),
                pl.BlockSpec((group, block, block), lambda g, *_: (g, 0, 0)),
            ],
            out_specs=(whole, whole),
            scratch_shapes=[pltpu.VMEM((th, rows, block), jnp.float32)],
        ),
        compiler_params=params(rows),
        cost_estimate=cost_us(10),
    )(meta, take, put, x, blocks)


def collect_kernel(th, group, flipped, parts, meta, take, put, *refs):
    h_refs = refs[:parts]
    w_ref, out_ref, acc = refs[parts:]
    g = pl.program_id(0)
    side = meta[0]
    block = w_ref.shape[-1]

    @pl.when(g == 0)
    def _():
        @pl.loop(0, acc.shape[0])
        def _(i):
            acc[i] = jnp.zeros(acc.shape[1:], jnp.float32)

    step = min(BATCH, group)

    def run(s, carry):
        products = []
        for j in range(step):
            i = slot_of(take[g * group + s * step + j], side, th)
            a = jnp.concatenate([h[i] for h in h_refs], axis=0)
            products.append(block_dot(a, w_ref[s * step + j], flipped))
        for j in range(step):
            acc[put[g * group + s * step + j]] += products[j]
        return carry

    lax.fori_loop(0, group // step, run, 0)

    @pl.when(g == pl.num_programs(0) - 1)
    def _():
        for t in range(acc.shape[0]):
            out_ref[:, t * block : (t + 1) * block] = acc[t].astype(jnp.bfloat16)


def collect(meta, hs, blocks, take, put, tw, flipped):
    th, _, block = hs[0].shape
    rows = sum(h.shape[1] for h in hs)
    nb = blocks.shape[0]
    group = min(GROUP, nb)
    return pl.pallas_call(
        functools.partial(collect_kernel, th, group, flipped, len(hs)),
        out_shape=jax.ShapeDtypeStruct((rows, tw * block), jnp.bfloat16),
        grid_spec=pltpu.PrefetchScalarGridSpec(
            num_scalar_prefetch=3,
            grid=(nb // group,),
            in_specs=[pl.BlockSpec(h.shape, lambda g, *_: (0, 0, 0)) for h in hs]
            + [pl.BlockSpec((group, block, block), lambda g, *_: (g, 0, 0))],
            out_specs=pl.BlockSpec((rows, tw * block), lambda g, *_: (0, 0)),
            scratch_shapes=[pltpu.VMEM((tw, rows, block), jnp.float32)],
        ),
        compiler_params=params(rows),
        cost_estimate=cost_us(30),
    )(meta, take, put, *hs, blocks)


def pack_kernel(size, meta, index, far_mid, far_out, near_own, near_out, full, *chosen):
    side, me, inner = meta[0], meta[2], meta[3]
    th = full.shape[0]
    half = th // 2

    @pl.when(inner == 1)
    def _():
        @pl.loop(0, half)
        def _(i):
            full[i] = far_mid[i]
            full[half + i] = near_own[i]

    @pl.when(inner == 0)
    def _():
        @pl.loop(0, half)
        def _(i):
            full[i] = far_out[i]
            full[half + i] = near_out[i]

    if size > 1:
        share = chosen[0].shape[0]
        step = min(4, share)

        @pl.loop(0, share // step)
        def _(b):
            for mask in range(1, size):
                base = jnp.bitwise_xor(me, mask) * share
                for j in range(step):
                    i = b * step + j
                    chosen[mask - 1][i] = full[slot_of(index[base + i], side, th)]


def pack(meta, index, far_mid, far_out, near_own, near_out, size):
    half, rows, block = near_own.shape
    share = index.shape[0] // size
    chosen = jax.ShapeDtypeStruct((share, rows, block), jnp.bfloat16)
    out = pl.pallas_call(
        functools.partial(pack_kernel, size),
        out_shape=(jax.ShapeDtypeStruct((2 * half, rows, block), jnp.bfloat16),)
        + (chosen,) * (size - 1),
        in_specs=[SMEM] * 2 + [VMEM] * 4,
        out_specs=(VMEM,) * size,
        compiler_params=params(rows),
        cost_estimate=cost(0, half * rows * block * 16),
    )(meta, index, far_mid, far_out, near_own, near_out)
    return out[0], out[1:]


def grads_kernel(th, chunks, widths, size, hidden_left, offset, meta, hid, wid, total, *refs):
    out = refs[-1]
    share, block, _ = out.shape
    side, me = meta[0], meta[2]
    hidden = [refs[m * chunks : (m + 1) * chunks] for m in range(size)]
    base = size * chunks
    width = [refs[base + m * widths : base + (m + 1) * widths] for m in range(size)]
    step = min(2, share)

    def run(b, carry):
        products = []
        for j in range(step):
            i = b * step + j
            k = me * share + i
            own = slot_of(hid[k], side, th)
            h = jnp.concatenate(
                [r[own if m == 0 else i] for m in range(size) for r in hidden[m]], axis=0
            )
            w = jnp.concatenate(
                [lanes(r, wid[k] + offset, block) for m in range(size) for r in width[m]], axis=0
            )
            a, c = (h, w) if hidden_left else (w, h)
            products.append(
                lax.dot_general(a, c, (((0,), (0,)), ((), ())), preferred_element_type=jnp.float32)
            )
        for j in range(step):
            out[b * step + j] = products[j] / total[0]
        return carry

    lax.fori_loop(0, share // step, run, 0)


def grads(meta, hidden, width, hidden_left, offset, hid, wid, total, size, th):
    block = hidden[0][0].shape[-1]
    share = hid.shape[0] // size
    rows = sum(w.shape[0] for w in width[0])
    flat = [r for group in hidden for r in group] + [r for group in width for r in group]
    return pl.pallas_call(
        functools.partial(
            grads_kernel, th, len(hidden[0]), len(width[0]), size, hidden_left, offset
        ),
        out_shape=jax.ShapeDtypeStruct((share, block, block), jnp.float32),
        in_specs=[SMEM] * 4 + [VMEM] * len(flat),
        out_specs=VMEM,
        compiler_params=params(rows),
        cost_estimate=cost_us(30),
    )(meta, hid, wid, total, *flat)


def prefix(values, d):
    return sum(jnp.where(e < d, v, 0) for e, v in enumerate(values))


def entry(values, d):
    return sum(jnp.where(e == d, v, 0) for e, v in enumerate(values))


class Plan:
    def __init__(self, every, cap):
        held = [(every[d] - 1) * PER_MB for d in range(every.shape[0])]
        self.held = held
        self.spare = [jnp.maximum(h - cap, 0) for h in held]
        self.owed = [jnp.maximum(cap - h, 0) for h in held]

    def span(self, lender, borrower):
        first, want = prefix(self.spare, lender), prefix(self.owed, borrower)
        low = jnp.maximum(first, want)
        high = jnp.minimum(first + entry(self.spare, lender), want + entry(self.owed, borrower))
        return low, high, first, want


def options_for(capacity):
    return [c for c in CAPACITIES if c * UNIT <= capacity - MB_TOK]


def most_lent(cap):
    return min(cap, SPARE - cap)


def lend_kernel(options, every, meta, tok, cot, *outs):
    size = every.shape[0]
    row, me = meta[1], meta[2]
    needed = (sum((every[d] - 1) * PER_MB for d in range(size)) + size - 1) // size
    cap = options[0]
    for small, large in zip(options[:-1], options[1:], strict=True):
        cap = cap + jnp.where(needed > small, large - small, 0)
    plan = Plan(every, cap)
    width = outs[0].shape[1] // 2
    column = pl.multiple_of(row * width, width)
    for mask in range(1, size):
        low, _, first, _ = plan.span(me, jnp.bitwise_xor(me, mask))
        out = outs[mask - 1]

        @pl.loop(0, out.shape[0] // UNIT)
        def _(s, out=out, low=low, first=first):
            unit = jnp.clip(cap + low + s - first, 0, SPARE - 1)
            rows = pl.ds(pl.multiple_of(MB_TOK + unit * UNIT, UNIT), UNIT)
            here = pl.ds(pl.multiple_of(s * UNIT, UNIT), UNIT)
            out[here, :width] = tok[rows, pl.ds(column, width)]
            out[here, width:] = cot[rows, pl.ds(column, width)]


def lend(every, meta, tok, cot, options, size, pieces):
    slots = max(most_lent(c) for c in options)
    shape = jax.ShapeDtypeStruct((slots * UNIT, 2 * tok.shape[1] // pieces), jnp.bfloat16)
    return pl.pallas_call(
        functools.partial(lend_kernel, options),
        out_shape=(shape,) * (size - 1),
        in_specs=[SMEM, SMEM, VMEM, VMEM],
        out_specs=(VMEM,) * (size - 1),
        compiler_params=params(),
        cost_estimate=cost(0, tok.size * 4),
    )(every, meta, tok, cot)


def borrow_kernel(cap, pieces, every, meta, tok, cot, *refs):
    out = refs[-1]
    lists = refs[:-1]
    row, me = meta[1], meta[2]
    plan = Plan(every, cap)
    held = entry(plan.held, me)
    whole = tok.shape[1]
    @pl.loop(0, cap)
    def _(i):
        here = pl.ds(pl.multiple_of(i * UNIT, UNIT), UNIT)
        there = pl.ds(pl.multiple_of(MB_TOK + i * UNIT, UNIT), UNIT)

        @pl.when(i < held)
        def _():
            out[here, :whole] = tok[there, :]
            out[here, whole:] = cot[there, :]

        @pl.when(i >= held)
        def _():
            out[here, :] = jnp.zeros((UNIT, 2 * whole), jnp.bfloat16)

    for n in range(len(lists) // pieces):
        low, high, _, want = plan.span(jnp.bitwise_xor(me, n + 1), me)
        width = lists[0].shape[1] // 2

        @pl.loop(0, cap)
        def _(i, n=n, low=low, high=high, want=want):
            at = want + i - held
            there = jnp.logical_and(i >= held, jnp.logical_and(at >= low, at < high))

            @pl.when(there)
            def _():
                rows = pl.ds(pl.multiple_of((at - low) * UNIT, UNIT), UNIT)
                here = pl.ds(pl.multiple_of(i * UNIT, UNIT), UNIT)
                for q in range(pieces):
                    column = pl.multiple_of(jnp.bitwise_xor(row, q) * width, width)
                    guest = lists[n * pieces + q]
                    out[here, pl.ds(column, width)] = guest[rows, :width]
                    out[here, pl.ds(column + whole, width)] = guest[rows, width:]


def borrow(every, meta, tok, cot, lists, cap, pieces):
    flat = [r for group in lists for r in group] if most_lent(cap) else []
    return pl.pallas_call(
        functools.partial(borrow_kernel, cap, pieces),
        out_shape=jax.ShapeDtypeStruct((cap * UNIT, 2 * tok.shape[1]), jnp.bfloat16),
        in_specs=[SMEM, SMEM] + [VMEM] * (2 + len(flat)),
        out_specs=VMEM,
        compiler_params=params(),
        cost_estimate=cost(0, tok.size * 4),
    )(every, meta, tok, cot, *flat)


def give_back_kernel(cap, every, meta, done, *outs):
    me = meta[2]
    plan = Plan(every, cap)
    held = entry(plan.held, me)
    for n, out in enumerate(outs):
        low, _, _, want = plan.span(jnp.bitwise_xor(me, n + 1), me)

        @pl.loop(0, out.shape[0] // UNIT)
        def _(s, out=out, low=low, want=want):
            unit = jnp.clip(held + low + s - want, 0, cap - 1)
            out[pl.ds(pl.multiple_of(s * UNIT, UNIT), UNIT), :] = unit_rows(done, unit)


def give_back(every, meta, done, cap, size):
    shape = jax.ShapeDtypeStruct((most_lent(cap) * UNIT, done.shape[1]), jnp.bfloat16)
    return pl.pallas_call(
        functools.partial(give_back_kernel, cap),
        out_shape=(shape,) * (size - 1),
        in_specs=[SMEM, SMEM, VMEM],
        out_specs=(VMEM,) * (size - 1),
        compiler_params=params(),
        cost_estimate=cost(0, done.size * 4),
    )(every, meta, done)


def settle_kernel(cap, every, meta, first_mb, extra, *refs):
    out = refs[-1]
    me = meta[2]
    plan = Plan(every, cap)
    held = entry(plan.held, me)
    width = out.shape[1]

    @pl.loop(0, PER_MB)
    def _(i):
        here = pl.ds(pl.multiple_of(i * UNIT, UNIT), UNIT)
        out[here, :] = first_mb[here, :]

    @pl.loop(0, (out.shape[0] - MB_TOK) // UNIT)
    def _(i):
        here = pl.ds(pl.multiple_of(MB_TOK + i * UNIT, UNIT), UNIT)
        own = jnp.logical_and(i < cap, i < held)

        @pl.when(own)
        def _():
            out[here, :] = unit_rows(extra, i)

        @pl.when(jnp.logical_not(own))
        def _():
            out[here, :] = jnp.zeros((UNIT, width), jnp.bfloat16)

    for n, guest in enumerate(refs[:-1]):
        low, high, first, _ = plan.span(me, jnp.bitwise_xor(me, n + 1))

        @pl.loop(cap, (out.shape[0] - MB_TOK) // UNIT)
        def _(i, guest=guest, low=low, high=high, first=first):
            at = first + i - cap
            there = jnp.logical_and(i < held, jnp.logical_and(at >= low, at < high))

            @pl.when(there)
            def _():
                here = pl.ds(pl.multiple_of(MB_TOK + i * UNIT, UNIT), UNIT)
                out[here, :] = unit_rows(guest, at - low)


def settle(every, meta, first_mb, extra, returned, cap, capacity):
    return pl.pallas_call(
        functools.partial(settle_kernel, cap),
        out_shape=jax.ShapeDtypeStruct((capacity, extra.shape[1]), jnp.bfloat16),
        in_specs=[SMEM, SMEM] + [VMEM] * (2 + len(returned)),
        out_specs=VMEM,
        compiler_params=params(),
        cost_estimate=cost(0, extra.size * 4),
    )(every, meta, first_mb, extra, *returned)


def over_row(x):
    return [x] + [swap(x, "row", q) for q in range(1, lax.axis_size("row"))]


def add_over_row(x):
    if lax.axis_size("row") == 2:
        return (x.astype(jnp.float32) + swap(x, "row", 1).astype(jnp.float32)).astype(x.dtype)
    return lax.psum(x.astype(jnp.float32), "row").astype(x.dtype)


def over_dp(x):
    return [swap(x, "dp", mask) for mask in range(1, lax.axis_size("dp"))]


def plus(*terms):
    return sum(t.astype(jnp.float32) for t in terms)


def branch(cap, capacity, th, tw, args):
    (every, meta, total, first, first_back, first_lists, first_rows, tokens, cotangent, up_tile,
     up_from, up_into, down_tile, down_from, down_into) = args
    size = lax.axis_size("dp")
    gather = size <= GATHER_MOST
    parts = size if gather else 1
    width = tokens.shape[1]
    pieces = lax.axis_size("row")
    rows = cap * UNIT

    def to_owners(chosen):
        return [swap(x, "dp", m + 1) for m, x in enumerate(chosen)]

    def to_all(x):
        return [swap(x, "dp", m) for m in range(1, size)] if gather else []

    def crossing(far, far_in):
        return along(plus(far, far_in).astype(jnp.bfloat16), MIDDLE)

    a_far, a_near = first_back
    a_sum = plus(*first)
    a_act = gelu_exact(a_sum).astype(jnp.bfloat16)
    a_far_in = along(a_far, INWARD)
    a_act_mid = along(a_act, MIDDLE)
    a_act_near = along(a_act, OUTWARD)

    extra = borrow(every, meta, tokens, cotangent, first_lists, cap, pieces)
    b_far, b_near = spread(
        meta, extra, (0, 0), rows, width, up_tile, up_from, up_into, th, False
    )
    b_far_in = along(b_far, INWARD)
    b_back_far, b_back_near = spread(
        meta, extra, (0, 1), rows, width, down_tile, down_into, down_from, th, True
    )

    a_act_far = along(a_act_mid, OUTWARD)
    a_near_in = along(tie(a_near, a_far_in, a_act_mid, a_act_near, b_far), INWARD)
    a_crossing = plus(a_far, a_far_in).astype(jnp.bfloat16)
    a_across = along(a_crossing, MIDDLE)

    b_near_in = along(tie(b_near, b_far_in, a_act_near), INWARD)
    b_across = crossing(b_far, tie(b_far_in, a_crossing))

    live = jnp.concatenate([first_rows, tie(extra, b_far)], axis=0)
    live_got = to_all(live)
    a_act_far = tie(a_act_far, *live_got)
    a_full, a_chosen = pack(meta, down_from, a_act_mid, a_act_far, a_act, a_act_near, parts)

    a_slope = gelu_slope(a_sum)
    a_grad = plus(a_near, a_near_in, tie(a_across, b_far_in, b_back_far, *a_chosen))
    a_grad = (a_grad * a_slope).astype(jnp.bfloat16)
    a_grad_mid = along(a_grad, MIDDLE)
    a_grad_near = along(a_grad, OUTWARD)

    a_y = collect(meta, [a_full], down_tile, down_from, down_into, tw, False)
    b_sum = plus(b_near, b_near_in, tie(b_across, a_grad, a_y))
    b_act = gelu_exact(b_sum).astype(jnp.bfloat16)
    b_act_mid = along(b_act, MIDDLE)
    b_act_near = along(b_act, OUTWARD)
    b_back_far_in = along(tie(b_back_far, b_near_in, b_across), INWARD)
    a_got = to_owners(a_chosen)

    a_grad_far = along(tie(a_grad_mid, a_grad_near, b_act), OUTWARD)

    b_act_far = along(tie(b_act_mid, a_grad_near), OUTWARD)
    b_back_near_in = along(tie(b_back_near, b_back_far_in, b_act_mid, *a_got), INWARD)
    b_back_across = crossing(b_back_far, b_back_far_in)

    a_hgrad, a_hchosen = pack(
        meta, up_into, a_grad_mid, a_grad_far, a_grad, a_grad_near, parts
    )
    b_grad = plus(b_back_near, b_back_near_in, tie(b_back_across, *a_hchosen))
    b_grad = (b_grad * gelu_slope(b_sum)).astype(jnp.bfloat16)
    b_grad_mid = along(b_grad, MIDDLE)
    b_grad_near = along(b_grad, OUTWARD)
    a_hgot = to_owners(a_hchosen)

    b_act_far = tie(b_act_far, b_grad_mid)
    b_full, b_chosen = pack(meta, down_from, b_act_mid, b_act_far, b_act, b_act_near, parts)
    b_grad_far = along(b_grad_mid, OUTWARD)
    b_got = to_owners(b_chosen)
    b_grad_far = tie(b_grad_far, *a_hgot)
    b_hgrad, b_hchosen = pack(
        meta, up_into, b_grad_mid, b_grad_far, b_grad, b_grad_near, parts
    )
    b_hgot = to_owners(b_hchosen)

    def finish(first_mb, b, blocks, take, put, flipped):
        first_mb = add_over_row(first_mb)
        rest = add_over_row(collect(meta, [b], blocks, take, put, tw, flipped))
        returned = []
        if most_lent(cap):
            sent = give_back(every, meta, tie(rest, *b_hgot[:1]), cap, size)
            returned = to_owners(sent)
        return settle(every, meta, first_mb, rest, returned, cap, capacity)

    rows_of = [[x] for x in [live] + live_got]

    def owned(a, b, a_got, b_got, hidden_left, offset, hid, wid):
        hidden = [[a, b]] + [list(g) for g in zip(a_got, b_got, strict=True)]
        if gather:
            return grads(meta, hidden, rows_of, hidden_left, offset, hid, wid, total, size, th)
        mine = grads(
            meta * jnp.array([1, 1, 0, 1], jnp.int32), hidden, rows_of, hidden_left, offset, hid,
            wid, jnp.ones_like(total), 1, th,
        )
        share = lax.psum_scatter(
            mine.astype(jnp.bfloat16), "dp", scatter_dimension=0, tiled=True
        )
        return share.astype(jnp.float32) / total[0]

    y_out = finish(a_y, tie(b_full, *b_hchosen), down_tile, down_from, down_into, False)
    grad_down = owned(tie(a_full, *b_hchosen), b_full, a_got, b_got, True, tw, down_from, down_into)
    b_hgrad_late = tie(b_hgrad, *b_hgot[:1])
    a_g = collect(meta, [tie(a_hgrad, *b_hchosen)], up_tile, up_into, up_from, tw, True)
    grad_tokens = finish(a_g, b_hgrad_late, up_tile, up_into, up_from, True)
    grad_up = owned(a_hgrad, b_hgrad, a_hgot, b_hgot, False, 0, up_into, up_from)
    return (y_out, grad_tokens, grad_up, grad_down)


def body(tokens, cotangent, counts, up_blocks, up_rows, up_cols, down_blocks, down_rows, down_cols):
    capacity, width = tokens.shape
    block = up_blocks.shape[-1]
    tw = width // block
    th = FF // lax.axis_size("row") // block
    size = lax.axis_size("dp")
    me = lax.axis_index("dp")
    up_tile, up_from, up_into = up_blocks[0, 0], up_rows[0, 0], up_cols[0, 0]
    down_tile, down_from, down_into = down_blocks[0, 0], down_rows[0, 0], down_cols[0, 0]
    col = lax.axis_index("col")
    inner = jnp.logical_or(col == 1, col == 2)
    meta = jnp.stack([col >= 2, lax.axis_index("row"), me, inner]).astype(jnp.int32)

    places = jnp.arange(size, dtype=jnp.int32)
    every = jnp.where(places == me, counts[0], 0)
    far, near = spread(meta, tokens, (0, 0), MB_TOK, width, up_tile, up_from, up_into, th, False)
    for bit in range(size.bit_length() - 1):
        every = every + swap(every if bit == 0 else tie(every, far), "dp", 1 << bit)

    far_in = along(far, INWARD)
    near_in = along(near, INWARD)
    across = along(plus(far, far_in).astype(jnp.bfloat16), MIDDLE)
    first_back = spread(
        meta, cotangent, (0, 0), MB_TOK, width, down_tile, down_into, down_from, th, True
    )

    first_rows = jnp.concatenate([tokens[:MB_TOK], cotangent[:MB_TOK]], axis=1)

    options = options_for(capacity)
    lent = lend(tie(every, *first_back), meta, tokens, cotangent, options, size, lax.axis_size("row"))
    lists = [over_row(swap(x, "dp", m + 1)) for m, x in enumerate(lent)]
    total = jnp.sum(every).astype(jnp.float32)[None]
    needed = (jnp.sum(every - 1) * PER_MB + size - 1) // size
    args = (every, meta, total, (near, near_in, across), first_back, lists, first_rows, tokens,
            cotangent, up_tile, up_from, up_into, down_tile, down_from, down_into)

    def choose(group, args):
        if len(group) == 1:
            return branch(group[0], capacity, th, tw, args)
        middle = len(group) // 2
        return lax.cond(
            needed > group[middle - 1],
            functools.partial(choose, group[middle:]),
            functools.partial(choose, group[:middle]),
            args,
        )

    y_out, grad_tokens, grad_up, grad_down = choose(options, args)
    return (y_out, grad_tokens, grad_up[None, None], grad_down[None, None])


def solution(mesh):
    return jax.shard_map(
        body,
        mesh=mesh,
        in_specs=(
            P("dp", "col"),
            P("dp", "col"),
            P("dp"),
            P("col", "row", None, None, None),
            P("col", "row", None),
            P("col", "row", None),
            P("row", "col", None, None, None),
            P("row", "col", None),
            P("row", "col", None),
        ),
        out_specs=(
            P("dp", "col"),
            P("dp", "col"),
            P("col", "row", "dp", None, None),
            P("row", "col", "dp", None, None),
        ),
        check_vma=False,
    )
```

```python
import functools

import jax
import jax.numpy as jnp
from jax import lax
from jax.experimental import pallas as pl
from jax.experimental.pallas import tpu as pltpu
from jax.sharding import PartitionSpec as P

FF = 16384
MB_TOK = 64
MB_MAX = 4
UNIT = 16
PER_MB = MB_TOK // UNIT
SPARE = (MB_MAX - 1) * PER_MB
BATCH = 8
GROUP = 64
VMEM_BASE = 8 * 1024 * 1024
VMEM_ROW = 64 * 1024
CAPACITIES = (3, 4, 5, 6, 8, 12)
GATHER_MOST = 4

SMEM = pl.BlockSpec(memory_space=pltpu.SMEM)
VMEM = pl.BlockSpec(memory_space=pltpu.VMEM)

INWARD = [(0, 1), (3, 2)]
MIDDLE = [(1, 2), (2, 1)]
OUTWARD = [(1, 0), (2, 3)]


def gelu_exact(hidden_in):
    return 0.5 * hidden_in * (1.0 + lax.erf(hidden_in * 0.7071067811865476))


def gelu_slope(hidden_in):
    normal_cdf = 0.5 * (1.0 + lax.erf(hidden_in * 0.7071067811865476))
    return normal_cdf + hidden_in * jnp.exp(-0.5 * hidden_in * hidden_in) * 0.3989422804014327


def swap(x, axis, mask):
    size = lax.axis_size(axis)
    return lax.ppermute(x, axis, [(i, i ^ mask) for i in range(size)])


def along(x, pairs):
    return lax.ppermute(x, "col", pairs)


def tie(x, *after):
    return lax.optimization_barrier((x, *after))[0]


def params(rows=64):
    return pltpu.CompilerParams(vmem_limit_bytes=VMEM_BASE + rows * VMEM_ROW)


def cost(flops, moved):
    return pl.CostEstimate(flops=flops, bytes_accessed=moved, transcendentals=0)


def cost_us(time):
    return cost(int(time * 1.1e9), 0)


def slot_of(index, side, count):
    moved = index + side * (count // 2)
    return jnp.where(moved >= count, moved - count, moved)


def lanes(ref, index, block):
    return ref[:, pl.ds(pl.multiple_of(index * block, block), block)]


def unit_rows(ref, unit, start=0):
    return ref[pl.ds(pl.multiple_of(start + unit * UNIT, UNIT), UNIT), :]


def block_dot(a, w, flipped):
    return lax.dot_general(
        a, w, (((1,), (1 if flipped else 0,)), ((), ())), preferred_element_type=jnp.float32
    )


def spread_kernel(th, group, flipped, meta, take, put, x_ref, w_ref, far_ref, near_ref, acc):
    g = pl.program_id(0)
    block = w_ref.shape[-1]
    half = th // 2
    side = meta[0]

    @pl.when(g == 0)
    def _():
        @pl.loop(0, acc.shape[0])
        def _(i):
            acc[i] = jnp.zeros(acc.shape[1:], jnp.float32)

    step = min(BATCH, group)

    def run(s, carry):
        products = []
        for j in range(step):
            a = lanes(x_ref, take[g * group + s * step + j], block)
            products.append(block_dot(a, w_ref[s * step + j], flipped))
        for j in range(step):
            o = slot_of(put[g * group + s * step + j], side, th)
            acc[o] += products[j]
        return carry

    lax.fori_loop(0, group // step, run, 0)

    @pl.when(g == pl.num_programs(0) - 1)
    def _():
        @pl.loop(0, half)
        def _(i):
            far_ref[i] = acc[i].astype(jnp.bfloat16)
            near_ref[i] = acc[half + i].astype(jnp.bfloat16)


def spread(meta, x, place, rows, width, blocks, take, put, th, flipped):
    nb, block, _ = blocks.shape
    group = min(GROUP, nb)
    shape = jax.ShapeDtypeStruct((th // 2, rows, block), jnp.bfloat16)
    whole = pl.BlockSpec((th // 2, rows, block), lambda g, *_: (0, 0, 0))
    return pl.pallas_call(
        functools.partial(spread_kernel, th, group, flipped),
        out_shape=(shape, shape),
        grid_spec=pltpu.PrefetchScalarGridSpec(
            num_scalar_prefetch=3,
            grid=(nb // group,),
            in_specs=[
                pl.BlockSpec((rows, width), lambda g, *_: place),
                pl.BlockSpec((group, block, block), lambda g, *_: (g, 0, 0)),
            ],
            out_specs=(whole, whole),
            scratch_shapes=[pltpu.VMEM((th, rows, block), jnp.float32)],
        ),
        compiler_params=params(rows),
        cost_estimate=cost_us(10),
    )(meta, take, put, x, blocks)


def collect_kernel(th, group, flipped, parts, meta, take, put, *refs):
    h_refs = refs[:parts]
    w_ref, out_ref, acc = refs[parts:]
    g = pl.program_id(0)
    side = meta[0]
    block = w_ref.shape[-1]

    @pl.when(g == 0)
    def _():
        @pl.loop(0, acc.shape[0])
        def _(i):
            acc[i] = jnp.zeros(acc.shape[1:], jnp.float32)

    step = min(BATCH, group)

    def run(s, carry):
        products = []
        for j in range(step):
            i = slot_of(take[g * group + s * step + j], side, th)
            a = jnp.concatenate([h[i] for h in h_refs], axis=0)
            products.append(block_dot(a, w_ref[s * step + j], flipped))
        for j in range(step):
            acc[put[g * group + s * step + j]] += products[j]
        return carry

    lax.fori_loop(0, group // step, run, 0)

    @pl.when(g == pl.num_programs(0) - 1)
    def _():
        for t in range(acc.shape[0]):
            out_ref[:, t * block : (t + 1) * block] = acc[t].astype(jnp.bfloat16)


def collect(meta, hs, blocks, take, put, tw, flipped):
    th, _, block = hs[0].shape
    rows = sum(h.shape[1] for h in hs)
    nb = blocks.shape[0]
    group = min(GROUP, nb)
    return pl.pallas_call(
        functools.partial(collect_kernel, th, group, flipped, len(hs)),
        out_shape=jax.ShapeDtypeStruct((rows, tw * block), jnp.bfloat16),
        grid_spec=pltpu.PrefetchScalarGridSpec(
            num_scalar_prefetch=3,
            grid=(nb // group,),
            in_specs=[pl.BlockSpec(h.shape, lambda g, *_: (0, 0, 0)) for h in hs]
            + [pl.BlockSpec((group, block, block), lambda g, *_: (g, 0, 0))],
            out_specs=pl.BlockSpec((rows, tw * block), lambda g, *_: (0, 0)),
            scratch_shapes=[pltpu.VMEM((tw, rows, block), jnp.float32)],
        ),
        compiler_params=params(rows),
        cost_estimate=cost_us(30),
    )(meta, take, put, *hs, blocks)


def pack_kernel(size, meta, index, far_mid, far_out, near_own, near_out, full, *chosen):
    side, me, inner = meta[0], meta[2], meta[3]
    th = full.shape[0]
    half = th // 2

    @pl.when(inner == 1)
    def _():
        @pl.loop(0, half)
        def _(i):
            full[i] = far_mid[i]
            full[half + i] = near_own[i]

    @pl.when(inner == 0)
    def _():
        @pl.loop(0, half)
        def _(i):
            full[i] = far_out[i]
            full[half + i] = near_out[i]

    if size > 1:
        share = chosen[0].shape[0]
        step = min(4, share)

        @pl.loop(0, share // step)
        def _(b):
            for mask in range(1, size):
                base = jnp.bitwise_xor(me, mask) * share
                for j in range(step):
                    i = b * step + j
                    chosen[mask - 1][i] = full[slot_of(index[base + i], side, th)]


def pack(meta, index, far_mid, far_out, near_own, near_out, size):
    half, rows, block = near_own.shape
    share = index.shape[0] // size
    chosen = jax.ShapeDtypeStruct((share, rows, block), jnp.bfloat16)
    out = pl.pallas_call(
        functools.partial(pack_kernel, size),
        out_shape=(jax.ShapeDtypeStruct((2 * half, rows, block), jnp.bfloat16),)
        + (chosen,) * (size - 1),
        in_specs=[SMEM] * 2 + [VMEM] * 4,
        out_specs=(VMEM,) * size,
        compiler_params=params(rows),
        cost_estimate=cost(0, half * rows * block * 16),
    )(meta, index, far_mid, far_out, near_own, near_out)
    return out[0], out[1:]


def grads_kernel(th, chunks, widths, size, hidden_left, offset, meta, hid, wid, total, *refs):
    out = refs[-1]
    share, block, _ = out.shape
    side, me = meta[0], meta[2]
    hidden = [refs[m * chunks : (m + 1) * chunks] for m in range(size)]
    base = size * chunks
    width = [refs[base + m * widths : base + (m + 1) * widths] for m in range(size)]
    step = min(2, share)

    def run(b, carry):
        products = []
        for j in range(step):
            i = b * step + j
            k = me * share + i
            own = slot_of(hid[k], side, th)
            h = jnp.concatenate(
                [r[own if m == 0 else i] for m in range(size) for r in hidden[m]], axis=0
            )
            w = jnp.concatenate(
                [lanes(r, wid[k] + offset, block) for m in range(size) for r in width[m]], axis=0
            )
            a, c = (h, w) if hidden_left else (w, h)
            products.append(
                lax.dot_general(a, c, (((0,), (0,)), ((), ())), preferred_element_type=jnp.float32)
            )
        for j in range(step):
            out[b * step + j] = products[j] / total[0]
        return carry

    lax.fori_loop(0, share // step, run, 0)


def grads(meta, hidden, width, hidden_left, offset, hid, wid, total, size, th):
    block = hidden[0][0].shape[-1]
    share = hid.shape[0] // size
    rows = sum(w.shape[0] for w in width[0])
    flat = [r for group in hidden for r in group] + [r for group in width for r in group]
    return pl.pallas_call(
        functools.partial(
            grads_kernel, th, len(hidden[0]), len(width[0]), size, hidden_left, offset
        ),
        out_shape=jax.ShapeDtypeStruct((share, block, block), jnp.float32),
        in_specs=[SMEM] * 4 + [VMEM] * len(flat),
        out_specs=VMEM,
        compiler_params=params(rows),
        cost_estimate=cost_us(30),
    )(meta, hid, wid, total, *flat)


def prefix(values, d):
    return sum(jnp.where(e < d, v, 0) for e, v in enumerate(values))


def entry(values, d):
    return sum(jnp.where(e == d, v, 0) for e, v in enumerate(values))


class Plan:
    def __init__(self, every, cap):
        held = [(every[d] - 1) * PER_MB for d in range(every.shape[0])]
        self.held = held
        self.spare = [jnp.maximum(h - cap, 0) for h in held]
        self.owed = [jnp.maximum(cap - h, 0) for h in held]

    def span(self, lender, borrower):
        first, want = prefix(self.spare, lender), prefix(self.owed, borrower)
        low = jnp.maximum(first, want)
        high = jnp.minimum(first + entry(self.spare, lender), want + entry(self.owed, borrower))
        return low, high, first, want


def options_for(capacity):
    return [c for c in CAPACITIES if c * UNIT <= capacity - MB_TOK]


def most_lent(cap):
    return min(cap, SPARE - cap)


def lend_kernel(options, every, meta, tok, cot, *outs):
    size = every.shape[0]
    row, me = meta[1], meta[2]
    needed = (sum((every[d] - 1) * PER_MB for d in range(size)) + size - 1) // size
    cap = options[0]
    for small, large in zip(options[:-1], options[1:], strict=True):
        cap = cap + jnp.where(needed > small, large - small, 0)
    plan = Plan(every, cap)
    width = outs[0].shape[1] // 2
    column = pl.multiple_of(row * width, width)
    for mask in range(1, size):
        low, _, first, _ = plan.span(me, jnp.bitwise_xor(me, mask))
        out = outs[mask - 1]

        @pl.loop(0, out.shape[0] // UNIT)
        def _(s, out=out, low=low, first=first):
            unit = jnp.clip(cap + low + s - first, 0, SPARE - 1)
            rows = pl.ds(pl.multiple_of(MB_TOK + unit * UNIT, UNIT), UNIT)
            here = pl.ds(pl.multiple_of(s * UNIT, UNIT), UNIT)
            out[here, :width] = tok[rows, pl.ds(column, width)]
            out[here, width:] = cot[rows, pl.ds(column, width)]


def lend(every, meta, tok, cot, options, size, pieces):
    slots = max(most_lent(c) for c in options)
    shape = jax.ShapeDtypeStruct((slots * UNIT, 2 * tok.shape[1] // pieces), jnp.bfloat16)
    return pl.pallas_call(
        functools.partial(lend_kernel, options),
        out_shape=(shape,) * (size - 1),
        in_specs=[SMEM, SMEM, VMEM, VMEM],
        out_specs=(VMEM,) * (size - 1),
        compiler_params=params(),
        cost_estimate=cost(0, tok.size * 4),
    )(every, meta, tok, cot)


def borrow_kernel(cap, pieces, every, meta, tok, cot, *refs):
    out = refs[-1]
    lists = refs[:-1]
    row, me = meta[1], meta[2]
    plan = Plan(every, cap)
    held = entry(plan.held, me)
    whole = tok.shape[1]
    @pl.loop(0, cap)
    def _(i):
        here = pl.ds(pl.multiple_of(i * UNIT, UNIT), UNIT)
        there = pl.ds(pl.multiple_of(MB_TOK + i * UNIT, UNIT), UNIT)

        @pl.when(i < held)
        def _():
            out[here, :whole] = tok[there, :]
            out[here, whole:] = cot[there, :]

        @pl.when(i >= held)
        def _():
            out[here, :] = jnp.zeros((UNIT, 2 * whole), jnp.bfloat16)

    for n in range(len(lists) // pieces):
        low, high, _, want = plan.span(jnp.bitwise_xor(me, n + 1), me)
        width = lists[0].shape[1] // 2

        @pl.loop(0, cap)
        def _(i, n=n, low=low, high=high, want=want):
            at = want + i - held
            there = jnp.logical_and(i >= held, jnp.logical_and(at >= low, at < high))

            @pl.when(there)
            def _():
                rows = pl.ds(pl.multiple_of((at - low) * UNIT, UNIT), UNIT)
                here = pl.ds(pl.multiple_of(i * UNIT, UNIT), UNIT)
                for q in range(pieces):
                    column = pl.multiple_of(jnp.bitwise_xor(row, q) * width, width)
                    guest = lists[n * pieces + q]
                    out[here, pl.ds(column, width)] = guest[rows, :width]
                    out[here, pl.ds(column + whole, width)] = guest[rows, width:]


def borrow(every, meta, tok, cot, lists, cap, pieces):
    flat = [r for group in lists for r in group] if most_lent(cap) else []
    return pl.pallas_call(
        functools.partial(borrow_kernel, cap, pieces),
        out_shape=jax.ShapeDtypeStruct((cap * UNIT, 2 * tok.shape[1]), jnp.bfloat16),
        in_specs=[SMEM, SMEM] + [VMEM] * (2 + len(flat)),
        out_specs=VMEM,
        compiler_params=params(),
        cost_estimate=cost(0, tok.size * 4),
    )(every, meta, tok, cot, *flat)


def give_back_kernel(cap, every, meta, done, *outs):
    me = meta[2]
    plan = Plan(every, cap)
    held = entry(plan.held, me)
    for n, out in enumerate(outs):
        low, _, _, want = plan.span(jnp.bitwise_xor(me, n + 1), me)

        @pl.loop(0, out.shape[0] // UNIT)
        def _(s, out=out, low=low, want=want):
            unit = jnp.clip(held + low + s - want, 0, cap - 1)
            out[pl.ds(pl.multiple_of(s * UNIT, UNIT), UNIT), :] = unit_rows(done, unit)


def give_back(every, meta, done, cap, size):
    shape = jax.ShapeDtypeStruct((most_lent(cap) * UNIT, done.shape[1]), jnp.bfloat16)
    return pl.pallas_call(
        functools.partial(give_back_kernel, cap),
        out_shape=(shape,) * (size - 1),
        in_specs=[SMEM, SMEM, VMEM],
        out_specs=(VMEM,) * (size - 1),
        compiler_params=params(),
        cost_estimate=cost(0, done.size * 4),
    )(every, meta, done)


def settle_kernel(cap, every, meta, first_mb, extra, *refs):
    out = refs[-1]
    me = meta[2]
    plan = Plan(every, cap)
    held = entry(plan.held, me)
    width = out.shape[1]

    @pl.loop(0, PER_MB)
    def _(i):
        here = pl.ds(pl.multiple_of(i * UNIT, UNIT), UNIT)
        out[here, :] = first_mb[here, :]

    @pl.loop(0, (out.shape[0] - MB_TOK) // UNIT)
    def _(i):
        here = pl.ds(pl.multiple_of(MB_TOK + i * UNIT, UNIT), UNIT)
        own = jnp.logical_and(i < cap, i < held)

        @pl.when(own)
        def _():
            out[here, :] = unit_rows(extra, i)

        @pl.when(jnp.logical_not(own))
        def _():
            out[here, :] = jnp.zeros((UNIT, width), jnp.bfloat16)

    for n, guest in enumerate(refs[:-1]):
        low, high, first, _ = plan.span(me, jnp.bitwise_xor(me, n + 1))

        @pl.loop(cap, (out.shape[0] - MB_TOK) // UNIT)
        def _(i, guest=guest, low=low, high=high, first=first):
            at = first + i - cap
            there = jnp.logical_and(i < held, jnp.logical_and(at >= low, at < high))

            @pl.when(there)
            def _():
                here = pl.ds(pl.multiple_of(MB_TOK + i * UNIT, UNIT), UNIT)
                out[here, :] = unit_rows(guest, at - low)


def settle(every, meta, first_mb, extra, returned, cap, capacity):
    return pl.pallas_call(
        functools.partial(settle_kernel, cap),
        out_shape=jax.ShapeDtypeStruct((capacity, extra.shape[1]), jnp.bfloat16),
        in_specs=[SMEM, SMEM] + [VMEM] * (2 + len(returned)),
        out_specs=VMEM,
        compiler_params=params(),
        cost_estimate=cost(0, extra.size * 4),
    )(every, meta, first_mb, extra, *returned)


def over_row(x):
    return [x] + [swap(x, "row", q) for q in range(1, lax.axis_size("row"))]


def add_over_row(x):
    if lax.axis_size("row") == 2:
        return (x.astype(jnp.float32) + swap(x, "row", 1).astype(jnp.float32)).astype(x.dtype)
    return lax.psum(x.astype(jnp.float32), "row").astype(x.dtype)


def over_dp(x):
    return [swap(x, "dp", mask) for mask in range(1, lax.axis_size("dp"))]


def plus(*terms):
    return sum(t.astype(jnp.float32) for t in terms)


def branch(cap, capacity, th, tw, args):
    (every, meta, total, first, first_back, first_lists, first_rows, tokens, cotangent, up_tile,
     up_from, up_into, down_tile, down_from, down_into) = args
    size = lax.axis_size("dp")
    gather = size <= GATHER_MOST
    parts = size if gather else 1
    width = tokens.shape[1]
    pieces = lax.axis_size("row")
    rows = cap * UNIT

    def to_owners(chosen):
        return [swap(x, "dp", m + 1) for m, x in enumerate(chosen)]

    def to_all(x):
        return [swap(x, "dp", m) for m in range(1, size)] if gather else []

    def crossing(far, far_in):
        return along(plus(far, far_in).astype(jnp.bfloat16), MIDDLE)

    a_far, a_near = first_back
    a_sum = plus(*first)
    a_act = gelu_exact(a_sum).astype(jnp.bfloat16)
    a_far_in = along(a_far, INWARD)
    a_act_mid = along(a_act, MIDDLE)
    a_act_near = along(a_act, OUTWARD)

    extra = borrow(every, meta, tokens, cotangent, first_lists, cap, pieces)
    b_far, b_near = spread(
        meta, extra, (0, 0), rows, width, up_tile, up_from, up_into, th, False
    )
    b_far_in = along(b_far, INWARD)
    b_back_far, b_back_near = spread(
        meta, extra, (0, 1), rows, width, down_tile, down_into, down_from, th, True
    )

    a_act_far = along(a_act_mid, OUTWARD)
    a_near_in = along(tie(a_near, a_far_in, a_act_mid, a_act_near, b_far), INWARD)
    a_crossing = plus(a_far, a_far_in).astype(jnp.bfloat16)
    a_across = along(a_crossing, MIDDLE)

    b_near_in = along(tie(b_near, b_far_in, a_act_near), INWARD)
    b_across = crossing(b_far, tie(b_far_in, a_crossing))

    live = jnp.concatenate([first_rows, tie(extra, b_far)], axis=0)
    live_got = to_all(live)
    a_act_far = tie(a_act_far, *live_got)
    a_full, a_chosen = pack(meta, down_from, a_act_mid, a_act_far, a_act, a_act_near, parts)

    a_slope = gelu_slope(a_sum)
    a_grad = plus(a_near, a_near_in, tie(a_across, b_far_in, b_back_far, *a_chosen))
    a_grad = (a_grad * a_slope).astype(jnp.bfloat16)
    a_grad_mid = along(a_grad, MIDDLE)
    a_grad_near = along(a_grad, OUTWARD)

    a_y = collect(meta, [a_full], down_tile, down_from, down_into, tw, False)
    b_sum = plus(b_near, b_near_in, tie(b_across, a_grad, a_y))
    b_act = gelu_exact(b_sum).astype(jnp.bfloat16)
    b_act_mid = along(b_act, MIDDLE)
    b_act_near = along(b_act, OUTWARD)
    b_back_far_in = along(tie(b_back_far, b_near_in, b_across), INWARD)
    a_got = to_owners(a_chosen)

    a_grad_far = along(tie(a_grad_mid, a_grad_near, b_act), OUTWARD)

    b_act_far = along(tie(b_act_mid, a_grad_near), OUTWARD)
    b_back_near_in = along(tie(b_back_near, b_back_far_in, b_act_mid, *a_got), INWARD)
    b_back_across = crossing(b_back_far, b_back_far_in)

    a_hgrad, a_hchosen = pack(
        meta, up_into, a_grad_mid, a_grad_far, a_grad, a_grad_near, parts
    )
    b_grad = plus(b_back_near, b_back_near_in, tie(b_back_across, *a_hchosen))
    b_grad = (b_grad * gelu_slope(b_sum)).astype(jnp.bfloat16)
    b_grad_mid = along(b_grad, MIDDLE)
    b_grad_near = along(b_grad, OUTWARD)
    a_hgot = to_owners(a_hchosen)

    b_act_far = tie(b_act_far, b_grad_mid)
    b_full, b_chosen = pack(meta, down_from, b_act_mid, b_act_far, b_act, b_act_near, parts)
    b_grad_far = along(b_grad_mid, OUTWARD)
    b_got = to_owners(b_chosen)
    b_grad_far = tie(b_grad_far, *a_hgot)
    b_hgrad, b_hchosen = pack(
        meta, up_into, b_grad_mid, b_grad_far, b_grad, b_grad_near, parts
    )
    b_hgot = to_owners(b_hchosen)

    def finish(first_mb, b, blocks, take, put, flipped):
        first_mb = add_over_row(first_mb)
        rest = add_over_row(collect(meta, [b], blocks, take, put, tw, flipped))
        returned = []
        if most_lent(cap):
            sent = give_back(every, meta, tie(rest, *b_hgot[:1]), cap, size)
            returned = to_owners(sent)
        return settle(every, meta, first_mb, rest, returned, cap, capacity)

    rows_of = [[x] for x in [live] + live_got]

    def owned(a, b, a_got, b_got, hidden_left, offset, hid, wid):
        hidden = [[a, b]] + [list(g) for g in zip(a_got, b_got, strict=True)]
        if gather:
            return grads(meta, hidden, rows_of, hidden_left, offset, hid, wid, total, size, th)
        mine = grads(
            meta * jnp.array([1, 1, 0, 1], jnp.int32), hidden, rows_of, hidden_left, offset, hid,
            wid, jnp.ones_like(total), 1, th,
        )
        share = lax.psum_scatter(
            mine.astype(jnp.bfloat16), "dp", scatter_dimension=0, tiled=True
        )
        return share.astype(jnp.float32) / total[0]

    y_out = finish(a_y, tie(b_full, *b_hchosen), down_tile, down_from, down_into, False)
    grad_down = owned(tie(a_full, *b_hchosen), b_full, a_got, b_got, True, tw, down_from, down_into)
    b_hgrad_late = tie(b_hgrad, *b_hgot[:1])
    a_g = collect(meta, [tie(a_hgrad, *b_hchosen)], up_tile, up_into, up_from, tw, True)
    grad_tokens = finish(a_g, b_hgrad_late, up_tile, up_into, up_from, True)
    grad_up = owned(a_hgrad, b_hgrad, a_hgot, b_hgot, False, 0, up_into, up_from)
    return (y_out, grad_tokens, grad_up, grad_down)


def body(tokens, cotangent, counts, up_blocks, up_rows, up_cols, down_blocks, down_rows, down_cols):
    capacity, width = tokens.shape
    block = up_blocks.shape[-1]
    tw = width // block
    th = FF // lax.axis_size("row") // block
    size = lax.axis_size("dp")
    me = lax.axis_index("dp")
    up_tile, up_from, up_into = up_blocks[0, 0], up_rows[0, 0], up_cols[0, 0]
    down_tile, down_from, down_into = down_blocks[0, 0], down_rows[0, 0], down_cols[0, 0]
    col = lax.axis_index("col")
    inner = jnp.logical_or(col == 1, col == 2)
    meta = jnp.stack([col >= 2, lax.axis_index("row"), me, inner]).astype(jnp.int32)

    places = jnp.arange(size, dtype=jnp.int32)
    every = jnp.where(places == me, counts[0], 0)
    far, near = spread(meta, tokens, (0, 0), MB_TOK, width, up_tile, up_from, up_into, th, False)
    for bit in range(size.bit_length() - 1):
        every = every + swap(every if bit == 0 else tie(every, far), "dp", 1 << bit)

    far_in = along(far, INWARD)
    near_in = along(near, INWARD)
    across = along(plus(far, far_in).astype(jnp.bfloat16), MIDDLE)
    first_back = spread(
        meta, cotangent, (0, 0), MB_TOK, width, down_tile, down_into, down_from, th, True
    )

    first_rows = jnp.concatenate([tokens[:MB_TOK], cotangent[:MB_TOK]], axis=1)

    options = options_for(capacity)
    lent = lend(tie(every, *first_back), meta, tokens, cotangent, options, size, lax.axis_size("row"))
    lists = [over_row(swap(x, "dp", m + 1)) for m, x in enumerate(lent)]
    total = jnp.sum(every).astype(jnp.float32)[None]
    needed = (jnp.sum(every - 1) * PER_MB + size - 1) // size
    args = (every, meta, total, (near, near_in, across), first_back, lists, first_rows, tokens,
            cotangent, up_tile, up_from, up_into, down_tile, down_from, down_into)

    def choose(group, args):
        if len(group) == 1:
            return branch(group[0], capacity, th, tw, args)
        return lax.cond(
            needed > group[0],
            functools.partial(choose, group[1:]),
            functools.partial(choose, group[:1]),
            args,
        )

    y_out, grad_tokens, grad_up, grad_down = choose(options, args)
    return (y_out, grad_tokens, grad_up[None, None], grad_down[None, None])


def solution(mesh):
    return jax.shard_map(
        body,
        mesh=mesh,
        in_specs=(
            P("dp", "col"),
            P("dp", "col"),
            P("dp"),
            P("col", "row", None, None, None),
            P("col", "row", None),
            P("col", "row", None),
            P("row", "col", None, None, None),
            P("row", "col", None),
            P("row", "col", None),
        ),
        out_specs=(
            P("dp", "col"),
            P("dp", "col"),
            P("col", "row", "dp", None, None),
            P("row", "col", "dp", None, None),
        ),
        check_vma=False,
    )
```

```python
import functools

import jax
import jax.numpy as jnp
from jax import lax
from jax.experimental import pallas as pl
from jax.experimental.pallas import tpu as pltpu
from jax.sharding import PartitionSpec as P

FF = 16384
MB_TOK = 64
MB_MAX = 4
UNIT = 16
PER_MB = MB_TOK // UNIT
SPARE = (MB_MAX - 1) * PER_MB
BATCH = 8
GROUP = 64
VMEM_BASE = 8 * 1024 * 1024
VMEM_ROW = 64 * 1024
CAPACITIES = (3, 4, 5, 6, 8, 12)
GATHER_MOST = 4

SMEM = pl.BlockSpec(memory_space=pltpu.SMEM)
VMEM = pl.BlockSpec(memory_space=pltpu.VMEM)

INWARD = [(0, 1), (3, 2)]
MIDDLE = [(1, 2), (2, 1)]
OUTWARD = [(1, 0), (2, 3)]


def gelu_exact(hidden_in):
    return 0.5 * hidden_in * (1.0 + lax.erf(hidden_in * 0.7071067811865476))


def gelu_slope(hidden_in):
    normal_cdf = 0.5 * (1.0 + lax.erf(hidden_in * 0.7071067811865476))
    return normal_cdf + hidden_in * jnp.exp(-0.5 * hidden_in * hidden_in) * 0.3989422804014327


def swap(x, axis, mask):
    size = lax.axis_size(axis)
    return lax.ppermute(x, axis, [(i, i ^ mask) for i in range(size)])


def along(x, pairs):
    return lax.ppermute(x, "col", pairs)


def tie(x, *after):
    return lax.optimization_barrier((x, *after))[0]


def params(rows=64):
    return pltpu.CompilerParams(vmem_limit_bytes=VMEM_BASE + rows * VMEM_ROW)


def cost(flops, moved):
    return pl.CostEstimate(flops=flops, bytes_accessed=moved, transcendentals=0)


def cost_us(time):
    return cost(int(time * 1.1e9), 0)


def slot_of(index, side, count):
    moved = index + side * (count // 2)
    return jnp.where(moved >= count, moved - count, moved)


def lanes(ref, index, block):
    return ref[:, pl.ds(pl.multiple_of(index * block, block), block)]


def unit_rows(ref, unit, start=0):
    return ref[pl.ds(pl.multiple_of(start + unit * UNIT, UNIT), UNIT), :]


def block_dot(a, w, flipped):
    return lax.dot_general(
        a, w, (((1,), (1 if flipped else 0,)), ((), ())), preferred_element_type=jnp.float32
    )


def spread_kernel(th, group, flipped, meta, take, put, x_ref, w_ref, far_ref, near_ref, acc):
    g = pl.program_id(0)
    block = w_ref.shape[-1]
    half = th // 2
    side = meta[0]

    @pl.when(g == 0)
    def _():
        @pl.loop(0, acc.shape[0])
        def _(i):
            acc[i] = jnp.zeros(acc.shape[1:], jnp.float32)

    step = min(BATCH, group)

    def run(s, carry):
        products = []
        for j in range(step):
            a = lanes(x_ref, take[g * group + s * step + j], block)
            products.append(block_dot(a, w_ref[s * step + j], flipped))
        for j in range(step):
            o = slot_of(put[g * group + s * step + j], side, th)
            acc[o] += products[j]
        return carry

    lax.fori_loop(0, group // step, run, 0)

    @pl.when(g == pl.num_programs(0) - 1)
    def _():
        @pl.loop(0, half)
        def _(i):
            far_ref[i] = acc[i].astype(jnp.bfloat16)
            near_ref[i] = acc[half + i].astype(jnp.bfloat16)


def spread(meta, x, place, rows, width, blocks, take, put, th, flipped):
    nb, block, _ = blocks.shape
    group = min(GROUP, nb)
    shape = jax.ShapeDtypeStruct((th // 2, rows, block), jnp.bfloat16)
    whole = pl.BlockSpec((th // 2, rows, block), lambda g, *_: (0, 0, 0))
    return pl.pallas_call(
        functools.partial(spread_kernel, th, group, flipped),
        out_shape=(shape, shape),
        grid_spec=pltpu.PrefetchScalarGridSpec(
            num_scalar_prefetch=3,
            grid=(nb // group,),
            in_specs=[
                pl.BlockSpec((rows, width), lambda g, *_: place),
                pl.BlockSpec((group, block, block), lambda g, *_: (g, 0, 0)),
            ],
            out_specs=(whole, whole),
            scratch_shapes=[pltpu.VMEM((th, rows, block), jnp.float32)],
        ),
        compiler_params=params(rows),
        cost_estimate=cost_us(10),
    )(meta, take, put, x, blocks)


def collect_kernel(th, group, flipped, parts, meta, take, put, *refs):
    h_refs = refs[:parts]
    w_ref, out_ref, acc = refs[parts:]
    g = pl.program_id(0)
    side = meta[0]
    block = w_ref.shape[-1]

    @pl.when(g == 0)
    def _():
        @pl.loop(0, acc.shape[0])
        def _(i):
            acc[i] = jnp.zeros(acc.shape[1:], jnp.float32)

    step = min(BATCH, group)

    def run(s, carry):
        products = []
        for j in range(step):
            i = slot_of(take[g * group + s * step + j], side, th)
            a = jnp.concatenate([h[i] for h in h_refs], axis=0)
            products.append(block_dot(a, w_ref[s * step + j], flipped))
        for j in range(step):
            acc[put[g * group + s * step + j]] += products[j]
        return carry

    lax.fori_loop(0, group // step, run, 0)

    @pl.when(g == pl.num_programs(0) - 1)
    def _():
        for t in range(acc.shape[0]):
            out_ref[:, t * block : (t + 1) * block] = acc[t].astype(jnp.bfloat16)


def collect(meta, hs, blocks, take, put, tw, flipped):
    th, _, block = hs[0].shape
    rows = sum(h.shape[1] for h in hs)
    nb = blocks.shape[0]
    group = min(GROUP, nb)
    return pl.pallas_call(
        functools.partial(collect_kernel, th, group, flipped, len(hs)),
        out_shape=jax.ShapeDtypeStruct((rows, tw * block), jnp.bfloat16),
        grid_spec=pltpu.PrefetchScalarGridSpec(
            num_scalar_prefetch=3,
            grid=(nb // group,),
            in_specs=[pl.BlockSpec(h.shape, lambda g, *_: (0, 0, 0)) for h in hs]
            + [pl.BlockSpec((group, block, block), lambda g, *_: (g, 0, 0))],
            out_specs=pl.BlockSpec((rows, tw * block), lambda g, *_: (0, 0)),
            scratch_shapes=[pltpu.VMEM((tw, rows, block), jnp.float32)],
        ),
        compiler_params=params(rows),
        cost_estimate=cost_us(30),
    )(meta, take, put, *hs, blocks)


def pack_kernel(size, meta, index, far_mid, far_out, near_own, near_out, full, *chosen):
    side, me, inner = meta[0], meta[2], meta[3]
    th = full.shape[0]
    half = th // 2

    @pl.when(inner == 1)
    def _():
        @pl.loop(0, half)
        def _(i):
            full[i] = far_mid[i]
            full[half + i] = near_own[i]

    @pl.when(inner == 0)
    def _():
        @pl.loop(0, half)
        def _(i):
            full[i] = far_out[i]
            full[half + i] = near_out[i]

    if size > 1:
        share = chosen[0].shape[0]
        step = min(4, share)

        @pl.loop(0, share // step)
        def _(b):
            for mask in range(1, size):
                base = jnp.bitwise_xor(me, mask) * share
                for j in range(step):
                    i = b * step + j
                    chosen[mask - 1][i] = full[slot_of(index[base + i], side, th)]


def pack(meta, index, far_mid, far_out, near_own, near_out, size):
    half, rows, block = near_own.shape
    share = index.shape[0] // size
    chosen = jax.ShapeDtypeStruct((share, rows, block), jnp.bfloat16)
    out = pl.pallas_call(
        functools.partial(pack_kernel, size),
        out_shape=(jax.ShapeDtypeStruct((2 * half, rows, block), jnp.bfloat16),)
        + (chosen,) * (size - 1),
        in_specs=[SMEM] * 2 + [VMEM] * 4,
        out_specs=(VMEM,) * size,
        compiler_params=params(rows),
        cost_estimate=cost(0, half * rows * block * 16),
    )(meta, index, far_mid, far_out, near_own, near_out)
    return out[0], out[1:]


def grads_kernel(th, chunks, widths, size, hidden_left, offset, meta, hid, wid, total, *refs):
    out = refs[-1]
    share, block, _ = out.shape
    side, me = meta[0], meta[2]
    hidden = [refs[m * chunks : (m + 1) * chunks] for m in range(size)]
    base = size * chunks
    width = [refs[base + m * widths : base + (m + 1) * widths] for m in range(size)]
    step = min(2, share)

    def run(b, carry):
        products = []
        for j in range(step):
            i = b * step + j
            k = me * share + i
            own = slot_of(hid[k], side, th)
            h = jnp.concatenate(
                [r[own if m == 0 else i] for m in range(size) for r in hidden[m]], axis=0
            )
            w = jnp.concatenate(
                [lanes(r, wid[k] + offset, block) for m in range(size) for r in width[m]], axis=0
            )
            a, c = (h, w) if hidden_left else (w, h)
            products.append(
                lax.dot_general(a, c, (((0,), (0,)), ((), ())), preferred_element_type=jnp.float32)
            )
        for j in range(step):
            out[b * step + j] = products[j] / total[0]
        return carry

    lax.fori_loop(0, share // step, run, 0)


def grads(meta, hidden, width, hidden_left, offset, hid, wid, total, size, th):
    block = hidden[0][0].shape[-1]
    share = hid.shape[0] // size
    rows = sum(w.shape[0] for w in width[0])
    flat = [r for group in hidden for r in group] + [r for group in width for r in group]
    return pl.pallas_call(
        functools.partial(
            grads_kernel, th, len(hidden[0]), len(width[0]), size, hidden_left, offset
        ),
        out_shape=jax.ShapeDtypeStruct((share, block, block), jnp.float32),
        in_specs=[SMEM] * 4 + [VMEM] * len(flat),
        out_specs=VMEM,
        compiler_params=params(rows),
        cost_estimate=cost_us(30),
    )(meta, hid, wid, total, *flat)


def prefix(values, d):
    return sum(jnp.where(e < d, v, 0) for e, v in enumerate(values))


def entry(values, d):
    return sum(jnp.where(e == d, v, 0) for e, v in enumerate(values))


class Plan:
    def __init__(self, every, cap):
        held = [(every[d] - 1) * PER_MB for d in range(every.shape[0])]
        self.held = held
        self.spare = [jnp.maximum(h - cap, 0) for h in held]
        self.owed = [jnp.maximum(cap - h, 0) for h in held]

    def span(self, lender, borrower):
        first, want = prefix(self.spare, lender), prefix(self.owed, borrower)
        low = jnp.maximum(first, want)
        high = jnp.minimum(first + entry(self.spare, lender), want + entry(self.owed, borrower))
        return low, high, first, want


def options_for(capacity):
    return [c for c in CAPACITIES if c * UNIT <= capacity - MB_TOK]


def most_lent(cap):
    return min(cap, SPARE - cap)


def lend_kernel(options, every, meta, tok, cot, *outs):
    size = every.shape[0]
    row, me = meta[1], meta[2]
    needed = (sum((every[d] - 1) * PER_MB for d in range(size)) + size - 1) // size
    cap = options[0]
    for small, large in zip(options[:-1], options[1:], strict=True):
        cap = cap + jnp.where(needed > small, large - small, 0)
    plan = Plan(every, cap)
    width = outs[0].shape[1] // 2
    column = pl.multiple_of(row * width, width)
    for mask in range(1, size):
        low, _, first, _ = plan.span(me, jnp.bitwise_xor(me, mask))
        out = outs[mask - 1]

        @pl.loop(0, out.shape[0] // UNIT)
        def _(s, out=out, low=low, first=first):
            unit = jnp.clip(cap + low + s - first, 0, SPARE - 1)
            rows = pl.ds(pl.multiple_of(MB_TOK + unit * UNIT, UNIT), UNIT)
            here = pl.ds(pl.multiple_of(s * UNIT, UNIT), UNIT)
            out[here, :width] = tok[rows, pl.ds(column, width)]
            out[here, width:] = cot[rows, pl.ds(column, width)]


def lend(every, meta, tok, cot, options, size, pieces):
    slots = max(most_lent(c) for c in options)
    shape = jax.ShapeDtypeStruct((slots * UNIT, 2 * tok.shape[1] // pieces), jnp.bfloat16)
    return pl.pallas_call(
        functools.partial(lend_kernel, options),
        out_shape=(shape,) * (size - 1),
        in_specs=[SMEM, SMEM, VMEM, VMEM],
        out_specs=(VMEM,) * (size - 1),
        compiler_params=params(),
        cost_estimate=cost(0, tok.size * 4),
    )(every, meta, tok, cot)


def borrow_kernel(cap, pieces, every, meta, tok, cot, *refs):
    out = refs[-1]
    lists = refs[:-1]
    row, me = meta[1], meta[2]
    plan = Plan(every, cap)
    held = entry(plan.held, me)
    whole = tok.shape[1]
    @pl.loop(0, cap)
    def _(i):
        here = pl.ds(pl.multiple_of(i * UNIT, UNIT), UNIT)
        there = pl.ds(pl.multiple_of(MB_TOK + i * UNIT, UNIT), UNIT)

        @pl.when(i < held)
        def _():
            out[here, :whole] = tok[there, :]
            out[here, whole:] = cot[there, :]

        @pl.when(i >= held)
        def _():
            out[here, :] = jnp.zeros((UNIT, 2 * whole), jnp.bfloat16)

    for n in range(len(lists) // pieces):
        low, high, _, want = plan.span(jnp.bitwise_xor(me, n + 1), me)
        width = lists[0].shape[1] // 2

        @pl.loop(0, cap)
        def _(i, n=n, low=low, high=high, want=want):
            at = want + i - held
            there = jnp.logical_and(i >= held, jnp.logical_and(at >= low, at < high))

            @pl.when(there)
            def _():
                rows = pl.ds(pl.multiple_of((at - low) * UNIT, UNIT), UNIT)
                here = pl.ds(pl.multiple_of(i * UNIT, UNIT), UNIT)
                for q in range(pieces):
                    column = pl.multiple_of(jnp.bitwise_xor(row, q) * width, width)
                    guest = lists[n * pieces + q]
                    out[here, pl.ds(column, width)] = guest[rows, :width]
                    out[here, pl.ds(column + whole, width)] = guest[rows, width:]


def borrow(every, meta, tok, cot, lists, cap, pieces):
    flat = [r for group in lists for r in group] if most_lent(cap) else []
    return pl.pallas_call(
        functools.partial(borrow_kernel, cap, pieces),
        out_shape=jax.ShapeDtypeStruct((cap * UNIT, 2 * tok.shape[1]), jnp.bfloat16),
        in_specs=[SMEM, SMEM] + [VMEM] * (2 + len(flat)),
        out_specs=VMEM,
        compiler_params=params(),
        cost_estimate=cost(0, tok.size * 4),
    )(every, meta, tok, cot, *flat)


def give_back_kernel(cap, every, meta, first, second, *outs):
    me = meta[2]
    plan = Plan(every, cap)
    held = entry(plan.held, me)
    width = first.shape[1]
    for n, out in enumerate(outs):
        low, _, _, want = plan.span(jnp.bitwise_xor(me, n + 1), me)

        @pl.loop(0, out.shape[0] // UNIT)
        def _(s, out=out, low=low, want=want):
            unit = jnp.clip(held + low + s - want, 0, cap - 1)
            here = pl.ds(pl.multiple_of(s * UNIT, UNIT), UNIT)
            out[here, :width] = unit_rows(first, unit)
            out[here, width:] = unit_rows(second, unit)


def give_back(every, meta, first, second, cap, size):
    shape = jax.ShapeDtypeStruct((most_lent(cap) * UNIT, 2 * first.shape[1]), jnp.bfloat16)
    return pl.pallas_call(
        functools.partial(give_back_kernel, cap),
        out_shape=(shape,) * (size - 1),
        in_specs=[SMEM, SMEM, VMEM, VMEM],
        out_specs=(VMEM,) * (size - 1),
        compiler_params=params(),
        cost_estimate=cost(0, first.size * 8),
    )(every, meta, first, second)


def settle_kernel(cap, every, meta, *refs):
    firsts, extras, outs = refs[:2], refs[2:4], refs[-2:]
    me = meta[2]
    plan = Plan(every, cap)
    held = entry(plan.held, me)
    capacity, width = outs[0].shape

    @pl.loop(0, PER_MB)
    def _(i):
        here = pl.ds(pl.multiple_of(i * UNIT, UNIT), UNIT)
        for first_mb, out in zip(firsts, outs, strict=True):
            out[here, :] = first_mb[here, :]

    @pl.loop(0, (capacity - MB_TOK) // UNIT)
    def _(i):
        here = pl.ds(pl.multiple_of(MB_TOK + i * UNIT, UNIT), UNIT)
        own = jnp.logical_and(i < cap, i < held)

        @pl.when(own)
        def _():
            for extra, out in zip(extras, outs, strict=True):
                out[here, :] = unit_rows(extra, i)

        @pl.when(jnp.logical_not(own))
        def _():
            for out in outs:
                out[here, :] = jnp.zeros((UNIT, width), jnp.bfloat16)

    for n, guest in enumerate(refs[4:-2]):
        low, high, first, _ = plan.span(me, jnp.bitwise_xor(me, n + 1))

        @pl.loop(cap, (capacity - MB_TOK) // UNIT)
        def _(i, guest=guest, low=low, high=high, first=first):
            at = first + i - cap
            there = jnp.logical_and(i < held, jnp.logical_and(at >= low, at < high))

            @pl.when(there)
            def _():
                here = pl.ds(pl.multiple_of(MB_TOK + i * UNIT, UNIT), UNIT)
                rows = unit_rows(guest, at - low)
                outs[0][here, :] = rows[:, :width]
                outs[1][here, :] = rows[:, width:]


def settle(every, meta, firsts, extras, returned, cap, capacity):
    shape = jax.ShapeDtypeStruct((capacity, extras[0].shape[1]), jnp.bfloat16)
    return pl.pallas_call(
        functools.partial(settle_kernel, cap),
        out_shape=(shape, shape),
        in_specs=[SMEM, SMEM] + [VMEM] * (4 + len(returned)),
        out_specs=(VMEM, VMEM),
        compiler_params=params(),
        cost_estimate=cost(0, extras[0].size * 8),
    )(every, meta, *firsts, *extras, *returned)


def over_row(x):
    return [x] + [swap(x, "row", q) for q in range(1, lax.axis_size("row"))]


def add_over_row(x):
    if lax.axis_size("row") == 2:
        return (x.astype(jnp.float32) + swap(x, "row", 1).astype(jnp.float32)).astype(x.dtype)
    return lax.psum(x.astype(jnp.float32), "row").astype(x.dtype)


def over_dp(x):
    return [swap(x, "dp", mask) for mask in range(1, lax.axis_size("dp"))]


def plus(*terms):
    return sum(t.astype(jnp.float32) for t in terms)


def branch(cap, capacity, th, tw, args):
    (every, meta, total, first, first_back, first_lists, first_rows, tokens, cotangent, up_tile,
     up_from, up_into, down_tile, down_from, down_into) = args
    size = lax.axis_size("dp")
    gather = size <= GATHER_MOST
    parts = size if gather else 1
    width = tokens.shape[1]
    pieces = lax.axis_size("row")
    rows = cap * UNIT

    def to_owners(chosen):
        return [swap(x, "dp", m + 1) for m, x in enumerate(chosen)]

    def to_all(x):
        return [swap(x, "dp", m) for m in range(1, size)] if gather else []

    def crossing(far, far_in):
        return along(plus(far, far_in).astype(jnp.bfloat16), MIDDLE)

    a_far, a_near = first_back
    a_sum = plus(*first)
    a_act = gelu_exact(a_sum).astype(jnp.bfloat16)
    a_far_in = along(a_far, INWARD)
    a_act_mid = along(a_act, MIDDLE)
    a_act_near = along(a_act, OUTWARD)

    extra = borrow(every, meta, tokens, cotangent, first_lists, cap, pieces)
    b_far, b_near = spread(
        meta, extra, (0, 0), rows, width, up_tile, up_from, up_into, th, False
    )
    b_far_in = along(b_far, INWARD)
    b_back_far, b_back_near = spread(
        meta, extra, (0, 1), rows, width, down_tile, down_into, down_from, th, True
    )

    a_act_far = along(a_act_mid, OUTWARD)
    a_near_in = along(tie(a_near, a_far_in, a_act_mid, a_act_near, b_far), INWARD)
    a_crossing = plus(a_far, a_far_in).astype(jnp.bfloat16)
    a_across = along(a_crossing, MIDDLE)

    b_near_in = along(tie(b_near, b_far_in, a_act_near), INWARD)
    b_across = crossing(b_far, tie(b_far_in, a_crossing))

    live = jnp.concatenate([first_rows, tie(extra, b_far)], axis=0)
    live_got = to_all(live)
    a_act_far = tie(a_act_far, *live_got)
    a_full, a_chosen = pack(meta, down_from, a_act_mid, a_act_far, a_act, a_act_near, parts)

    a_slope = gelu_slope(a_sum)
    a_grad = plus(a_near, a_near_in, tie(a_across, b_far_in, b_back_far, *a_chosen))
    a_grad = (a_grad * a_slope).astype(jnp.bfloat16)
    a_grad_mid = along(a_grad, MIDDLE)
    a_grad_near = along(a_grad, OUTWARD)

    a_y = collect(meta, [a_full], down_tile, down_from, down_into, tw, False)
    b_sum = plus(b_near, b_near_in, tie(b_across, a_grad, a_y))
    b_act = gelu_exact(b_sum).astype(jnp.bfloat16)
    b_act_mid = along(b_act, MIDDLE)
    b_act_near = along(b_act, OUTWARD)
    b_back_far_in = along(tie(b_back_far, b_near_in, b_across), INWARD)
    a_got = to_owners(a_chosen)

    a_grad_far = along(tie(a_grad_mid, a_grad_near, b_act), OUTWARD)

    b_act_far = along(tie(b_act_mid, a_grad_near), OUTWARD)
    b_back_near_in = along(tie(b_back_near, b_back_far_in, b_act_mid, *a_got), INWARD)
    b_back_across = crossing(b_back_far, b_back_far_in)

    a_hgrad, a_hchosen = pack(
        meta, up_into, a_grad_mid, a_grad_far, a_grad, a_grad_near, parts
    )
    b_grad = plus(b_back_near, b_back_near_in, tie(b_back_across, *a_hchosen))
    b_grad = (b_grad * gelu_slope(b_sum)).astype(jnp.bfloat16)
    b_grad_mid = along(b_grad, MIDDLE)
    b_grad_near = along(b_grad, OUTWARD)
    a_hgot = to_owners(a_hchosen)

    b_act_far = tie(b_act_far, b_grad_mid)
    b_full, b_chosen = pack(meta, down_from, b_act_mid, b_act_far, b_act, b_act_near, parts)
    b_grad_far = along(b_grad_mid, OUTWARD)
    b_got = to_owners(b_chosen)
    b_y = collect(
        meta, [tie(b_full, *a_hgot[:1])], down_tile, down_from, down_into, tw, False
    )
    b_grad_far = tie(b_grad_far, b_y, *a_hgot)
    b_hgrad, b_hchosen = pack(
        meta, up_into, b_grad_mid, b_grad_far, b_grad, b_grad_near, parts
    )
    b_hgot = to_owners(b_hchosen)

    rows_of = [[x] for x in [live] + live_got]

    def owned(a, b, a_got, b_got, hidden_left, offset, hid, wid):
        hidden = [[a, b]] + [list(g) for g in zip(a_got, b_got, strict=True)]
        if gather:
            return grads(meta, hidden, rows_of, hidden_left, offset, hid, wid, total, size, th)
        mine = grads(
            meta * jnp.array([1, 1, 0, 1], jnp.int32), hidden, rows_of, hidden_left, offset, hid,
            wid, jnp.ones_like(total), 1, th,
        )
        share = lax.psum_scatter(
            mine.astype(jnp.bfloat16), "dp", scatter_dimension=0, tiled=True
        )
        return share.astype(jnp.float32) / total[0]

    a_g = collect(meta, [tie(a_hgrad, *b_hchosen)], up_tile, up_into, up_from, tw, True)
    b_g = collect(
        meta, [tie(b_hgrad, *b_hgot[:1])], up_tile, up_into, up_from, tw, True
    )
    y_first, y_rest = add_over_row(a_y), add_over_row(b_y)
    g_first, g_rest = add_over_row(a_g), add_over_row(b_g)
    sent = give_back(every, meta, y_rest, g_rest, cap, size) if most_lent(cap) else ()
    returned = to_owners(sent)
    grad_down = owned(tie(a_full, a_g), b_full, a_got, b_got, True, tw, down_from, down_into)
    y_out, grad_tokens = settle(
        every, meta, (y_first, g_first), (y_rest, g_rest), returned, cap, capacity
    )
    grad_up = owned(tie(a_hgrad, grad_down), b_hgrad, a_hgot, b_hgot, False, 0, up_into, up_from)
    return (y_out, grad_tokens, grad_up, grad_down)


def body(tokens, cotangent, counts, up_blocks, up_rows, up_cols, down_blocks, down_rows, down_cols):
    capacity, width = tokens.shape
    block = up_blocks.shape[-1]
    tw = width // block
    th = FF // lax.axis_size("row") // block
    size = lax.axis_size("dp")
    me = lax.axis_index("dp")
    up_tile, up_from, up_into = up_blocks[0, 0], up_rows[0, 0], up_cols[0, 0]
    down_tile, down_from, down_into = down_blocks[0, 0], down_rows[0, 0], down_cols[0, 0]
    col = lax.axis_index("col")
    inner = jnp.logical_or(col == 1, col == 2)
    meta = jnp.stack([col >= 2, lax.axis_index("row"), me, inner]).astype(jnp.int32)

    places = jnp.arange(size, dtype=jnp.int32)
    every = jnp.where(places == me, counts[0], 0)
    far, near = spread(meta, tokens, (0, 0), MB_TOK, width, up_tile, up_from, up_into, th, False)
    for bit in range(size.bit_length() - 1):
        every = every + swap(every if bit == 0 else tie(every, far), "dp", 1 << bit)

    far_in = along(far, INWARD)
    near_in = along(near, INWARD)
    across = along(plus(far, far_in).astype(jnp.bfloat16), MIDDLE)
    first_back = spread(
        meta, cotangent, (0, 0), MB_TOK, width, down_tile, down_into, down_from, th, True
    )

    first_rows = jnp.concatenate([tokens[:MB_TOK], cotangent[:MB_TOK]], axis=1)

    options = options_for(capacity)
    lent = lend(tie(every, *first_back), meta, tokens, cotangent, options, size, lax.axis_size("row"))
    lists = [over_row(swap(x, "dp", m + 1)) for m, x in enumerate(lent)]
    total = jnp.sum(every).astype(jnp.float32)[None]
    needed = (jnp.sum(every - 1) * PER_MB + size - 1) // size
    args = (every, meta, total, (near, near_in, across), first_back, lists, first_rows, tokens,
            cotangent, up_tile, up_from, up_into, down_tile, down_from, down_into)

    def choose(group, args):
        if len(group) == 1:
            return branch(group[0], capacity, th, tw, args)
        return lax.cond(
            needed > group[0],
            functools.partial(choose, group[1:]),
            functools.partial(choose, group[:1]),
            args,
        )

    y_out, grad_tokens, grad_up, grad_down = choose(options, args)
    return (y_out, grad_tokens, grad_up[None, None], grad_down[None, None])


def solution(mesh):
    return jax.shard_map(
        body,
        mesh=mesh,
        in_specs=(
            P("dp", "col"),
            P("dp", "col"),
            P("dp"),
            P("col", "row", None, None, None),
            P("col", "row", None),
            P("col", "row", None),
            P("row", "col", None, None, None),
            P("row", "col", None),
            P("row", "col", None),
        ),
        out_specs=(
            P("dp", "col"),
            P("dp", "col"),
            P("col", "row", "dp", None, None),
            P("row", "col", "dp", None, None),
        ),
        check_vma=False,
    )
```
